32 devices in a mesh: seq: 4 (over y, x), head: 4 (over z), batch: 2 (over core).
Axes of the slice: x: 2, y: 2, z: 4, core: 2. Of those that a mesh axis runs over, the one named last changes fastest.
Arguments:
- queries: bfloat16 [16384, 1024], P(('batch', 'seq'), 'head'), parts along dimension 0, may hold values from -6 to 6
- keys: bfloat16 [16384, 1024], P(('batch', 'seq'), 'head'), parts along dimension 0, may hold values from -6 to 6
- values: bfloat16 [16384, 1024], P(('batch', 'seq'), 'head'), parts along dimension 0, may hold values from -6 to 6
- rand_blocks: int32 [256, 16, 3], P(('batch', 'seq'), 'head'), parts along dimension 0, may hold values from 0 to 127, as said below
- global_blocks: int32 [16], P(('batch', 'seq')), parts along dimension 0, may hold values from 0 to 127, as said below
Outputs:
- attended: bfloat16 [16384, 1024], P(('batch', 'seq'), 'head'), parts along dimension 0
The draws below stay inside these ranges and needn't reach their ends.
There are 2 independent parts, one for each index of `batch`. The reference program is written for one: setup_inputs(seed, part) draws one part's arguments, and reference() takes and returns one part's arrays. A program takes and returns all parts, laid end to end along the dimension named above; each array names one. Nothing has to cross between parts.
Inputs may be any that keep to these rules, and one draw needn't show every extreme that they name: `rand_blocks`: over the 32 block rows of one device's range and one head, the random blocks that lie in any one device's range of 32 blocks are exactly 24 distinct blocks. `global_blocks`: entries 2i and 2i+1 are two distinct blocks of device i's range, from i * 32 to (i + 1) * 32 - 1.
All inputs are finite; a program needn't handle non-finite values.
Results may differ from the reference program's by a relative error of at most 0.0041.
Values may be sent and summed in bfloat16 or wider, within the bound.
No kernel may reach another device: no remote copies, remote signals or barrier semaphores. Data moves between devices by JAX's collectives and lax.ppermute only.
A program may use at most 192 MiB of HBM per device.

```python
import jax
import jax.numpy as jnp
from jax import lax

H = 16
DH = 64
BLK = 64
RAND = 3
GPD = 2
S_DEV = 2048
NB_DEV = 32
L = 8192
NB = 128
CAP = 24
N_SEQ = 4


def draw_queries(key, part):
    field = jnp.clip(1.5 * jax.random.normal(jax.random.fold_in(key, 1), (NB, BLK, H, DH), jnp.float32), -6.0, 6.0)
    return field.reshape(NB * BLK, H * DH).astype(jnp.bfloat16)


def draw_keys(key, part):
    field = jnp.clip(jax.random.normal(jax.random.fold_in(key, 2), (NB, BLK, H, DH), jnp.float32), -6.0, 6.0)
    return field.reshape(NB * BLK, H * DH).astype(jnp.bfloat16)


def draw_rand_blocks(key, part):
    pair_keys = jax.random.split(key, N_SEQ * H)
    total_cands = N_SEQ * CAP

    def per_pair(pair_key):
        sub_keys = jax.random.split(pair_key, N_SEQ + 2)
        firsts = jax.vmap(lambda owner_key: jax.random.permutation(owner_key, NB_DEV)[:CAP])(sub_keys[:N_SEQ])
        cands = (firsts + (jnp.arange(N_SEQ, dtype=jnp.int32) * NB_DEV)[:, None]).reshape(-1)
        extra_pos = jax.random.randint(sub_keys[N_SEQ], (NB_DEV * RAND - total_cands,), 0, total_cands)
        picks = jnp.concatenate([cands, cands[extra_pos]])
        picks = jax.random.permutation(sub_keys[N_SEQ + 1], picks)
        return picks.reshape(NB_DEV, RAND)
    result = jax.vmap(per_pair)(pair_keys).reshape(N_SEQ, H, NB_DEV, RAND)
    return result.transpose(0, 2, 1, 3).reshape(NB, H, RAND).astype(jnp.int32)


def draw_global_blocks(key, part):
    dev_keys = jax.random.split(jax.random.fold_in(key, 11), N_SEQ)
    firsts = jax.vmap(lambda dev_key: jax.random.permutation(dev_key, NB_DEV)[:GPD])(dev_keys)
    result = firsts + (jnp.arange(N_SEQ, dtype=jnp.int32) * NB_DEV)[:, None]
    return result.reshape(-1).astype(jnp.int32)


def block_levels(key, extent, cuts, low, high):
    def one(position, shards_of):
        draws = jax.random.uniform(jax.random.fold_in(jax.random.fold_in(key, 6), position), (shards_of,), jnp.float32, low / len(cuts), high / len(cuts))
        return jnp.repeat(jnp.exp(draws), extent[position] // shards_of).reshape((-1,) + (1,) * (len(extent) - position - 1))

    loudness = one(*cuts[0])
    for cut in cuts[1:]:
        loudness = loudness * one(*cut)
    return loudness


def noise(key, extent, spread, limit, pieces=(), kind=jnp.bfloat16):
    entries = jax.random.normal(key, extent, jnp.float32) * spread
    if len(pieces) > 0:
        entries = block_levels(key, extent, pieces, -0.22, 0.18) * entries
    return jnp.clip(entries, min=-limit, max=limit).astype(kind)


def setup_inputs(seed: int = 0, part: int = 0) -> dict:
    key_of = jax.random.split(jax.random.key(seed), 6)
    part_splits = jax.random.split(jax.random.fold_in(key_of[5], part), 6)
    return {
        "queries": draw_queries(jax.random.fold_in(jax.random.fold_in(key_of[5], part), 71), part),
        "keys": draw_keys(jax.random.fold_in(jax.random.fold_in(key_of[5], part), 71), part),
        "values": noise(part_splits[2], (L, H * DH), 1.0, 6.0, ((0, 4), (1, 4))),
        "rand_blocks": draw_rand_blocks(jax.random.fold_in(jax.random.fold_in(key_of[5], part), 71), part),
        "global_blocks": draw_global_blocks(jax.random.fold_in(jax.random.fold_in(key_of[5], part), 71), part),
    }


score_scale = 0.125


def attend(query_blk, window_kv, random_kv, global_kv):
    rows = query_blk.shape[0]
    qf = query_blk.astype(jnp.float32)
    wf = window_kv.astype(jnp.float32)
    rf = random_kv.astype(jnp.float32)
    gf = global_kv.astype(jnp.float32)
    s_win = jnp.einsum("rqd,rjkd->rqjk", qf, wf[..., :DH]).reshape(rows, BLK, -1)
    s_rnd = jnp.einsum("rqd,rjkd->rqjk", qf, rf[..., :DH]).reshape(rows, BLK, -1)
    s_glb = jnp.einsum("rqd,gkd->rqgk", qf, gf[..., :DH]).reshape(rows, BLK, -1)
    scores = jnp.concatenate([s_win, s_rnd, s_glb], axis=-1) * score_scale
    peak = jnp.max(scores, axis=-1, keepdims=True)
    weights = jnp.exp(scores - peak)
    totals = jnp.sum(weights, axis=-1)
    probs = weights.astype(jnp.bfloat16).astype(jnp.float32)
    span = 3 * BLK
    p_win = probs[..., :span].reshape(rows, BLK, 3, BLK)
    p_rnd = probs[..., span:2 * span].reshape(rows, BLK, 3, BLK)
    p_glb = probs[..., 2 * span:].reshape(rows, BLK, -1, BLK)
    summed = jnp.einsum("rqjk,rjkd->rqd", p_win, wf[..., DH:])
    summed = summed + jnp.einsum("rqjk,rjkd->rqd", p_rnd, rf[..., DH:])
    summed = summed + jnp.einsum("rqgk,gkd->rqd", p_glb, gf[..., DH:])
    return (summed / totals[..., None]).astype(jnp.bfloat16)


def global_rows(glob_query, head_kv):
    flat_q = glob_query.reshape(-1, DH)
    ranges = head_kv.reshape(N_SEQ, S_DEV, 2 * DH)

    def one_range(range_kv):
        scores = jnp.dot(flat_q, range_kv[:, :DH].T, preferred_element_type=jnp.float32) * score_scale
        peak = jnp.max(scores, axis=1)
        weights = jnp.exp(scores - peak[:, None])
        totals = jnp.sum(weights, axis=1)
        summed = jnp.dot(weights.astype(jnp.bfloat16), range_kv[:, DH:], preferred_element_type=jnp.float32)
        return peak, totals, summed

    peaks, totals, sums = lax.map(one_range, ranges)
    top = jnp.max(peaks, axis=0)
    factor = jnp.exp(peaks - top[None, :])
    whole_totals = jnp.sum(factor * totals, axis=0)
    whole_sums = jnp.sum(factor[..., None] * sums, axis=0)
    return (whole_sums / whole_totals[:, None]).astype(jnp.bfloat16).reshape(glob_query.shape)


def reference(queries, keys, values, rand_blocks, global_blocks):
    q_heads = queries.reshape(NB, BLK, H, DH).transpose(2, 0, 1, 3)
    kv_heads = jnp.concatenate([keys.reshape(NB, BLK, H, DH), values.reshape(NB, BLK, H, DH)], axis=-1).transpose(2, 0, 1, 3)
    rand_heads = rand_blocks.transpose(1, 0, 2)

    def per_head(items):
        q_head, kv_head, rand_head = items
        window_kv = jnp.stack([jnp.roll(kv_head, 1, axis=0), kv_head, jnp.roll(kv_head, -1, axis=0)], axis=1)
        random_kv = kv_head[rand_head]
        global_kv = kv_head[global_blocks]
        sparse = attend(q_head, window_kv, random_kv, global_kv)
        glob_out = global_rows(q_head[global_blocks], kv_head)
        return sparse.at[global_blocks].set(glob_out)

    result = lax.map(per_head, (q_heads, kv_heads, rand_heads))
    return result.transpose(1, 2, 0, 3).reshape(L, H * DH)
```

```python
import functools

import jax
import jax.numpy as jnp
from jax import lax
from jax.experimental import pallas as pl
from jax.experimental.pallas import tpu as pltpu
from jax.sharding import PartitionSpec as P

DH = 64
BLK = 64
RAND = 3
LANES = 2 * DH
ROWS = 2
CHUNK = 512
EXP2_SCALE = 0.125 * 1.4426950408889634


def qk(q, k):
    return lax.dot_general(q, k, (((1,), (1,)), ((), ())), preferred_element_type=jnp.float32)


def pv(p, v):
    return jnp.dot(p.astype(jnp.bfloat16), v, preferred_element_type=jnp.float32)


def pair_kernel(
    pair, ranges, gpd, tokens, rand_ref, win_ref, glob_ref, own_ref, q_ref, *refs
):
    k_refs, v_refs, refs = refs[:ranges], refs[ranges : 2 * ranges], refs[2 * ranges :]
    if pair > 0:
        refs = refs[1:]
    out_ref, k_all, v_all, k_glob, v_glob, sems = refs
    blocks = tokens // BLK
    globs = gpd * ranges

    def view(ref, j):
        return ref.at[:, pl.ds(pair * LANES, LANES)] if j == 0 else ref

    copies = []
    for j in range(ranges):
        span = pl.ds(j * tokens, tokens)
        copies.append(pltpu.make_async_copy(view(k_refs[j], j), k_all.at[span], sems.at[2 * j]))
        copies.append(pltpu.make_async_copy(view(v_refs[j], j), v_all.at[span], sems.at[2 * j + 1]))
    for copy in copies:
        copy.start()
    for copy in copies:
        copy.wait()

    first = lax.broadcasted_iota(jnp.int32, (BLK, LANES), 1) < DH

    def split_heads(q):
        zero = jnp.zeros_like(q)
        return [jnp.where(first, q, zero), jnp.where(first, zero, q)]

    def block(ref, position):
        return ref[pl.ds(pl.multiple_of(position * BLK, BLK), BLK), :]

    def finish(summed, totals):
        o = summed * (1.0 / totals)
        return jnp.where(first, o[:BLK], o[BLK:]).astype(jnp.bfloat16)

    for g in range(globs):
        k_glob[g * BLK : (g + 1) * BLK, :] = block(k_all, glob_ref[g])
        v_glob[g * BLK : (g + 1) * BLK, :] = block(v_all, glob_ref[g])

    def rows_step(step, carry):
        base = step * ROWS
        q_bd, listed = [], []
        for u in range(ROWS):
            b = base + u
            q_bd += split_heads(block(q_ref, b))
            k_list, v_list = [], []
            for j in range(3):
                k_list.append(block(k_all, win_ref[b + j]))
                v_list.append(block(v_all, win_ref[b + j]))
            for j in range(RAND):
                at_a = rand_ref[b * 2 * RAND + j]
                at_b = rand_ref[b * 2 * RAND + RAND + j]
                k_list.append(jnp.where(first, block(k_all, at_a), block(k_all, at_b)))
                v_list.append(jnp.where(first, block(v_all, at_a), block(v_all, at_b)))
            listed.append((jnp.concatenate(k_list, axis=0), jnp.concatenate(v_list, axis=0)))
        q_bd = jnp.concatenate(q_bd, axis=0)
        s_own = jnp.concatenate(
            [qk(q_bd[2 * BLK * u : 2 * BLK * (u + 1)], listed[u][0]) for u in range(ROWS)], axis=0
        )
        s_glob = qk(q_bd, k_glob[...])
        peak = jnp.maximum(
            jnp.max(s_own, axis=1, keepdims=True), jnp.max(s_glob, axis=1, keepdims=True)
        )
        w_own = jnp.exp2((s_own - peak) * EXP2_SCALE)
        w_glob = jnp.exp2((s_glob - peak) * EXP2_SCALE)
        totals = jnp.sum(w_own, axis=1, keepdims=True) + jnp.sum(w_glob, axis=1, keepdims=True)
        o_glob = pv(w_glob, v_glob[...])
        for u in range(ROWS):
            part = slice(2 * BLK * u, 2 * BLK * (u + 1))
            o = o_glob[part] + pv(w_own[part], listed[u][1])
            where = pl.ds(pl.multiple_of((base + u) * BLK, BLK), BLK)
            out_ref[where, :] = finish(o, totals[part])
        return carry

    lax.fori_loop(0, blocks // ROWS, rows_step, 0)

    q_glob = []
    for g in range(gpd):
        q_glob += split_heads(block(q_ref, own_ref[g]))
    q_glob = jnp.concatenate(q_glob, axis=0)

    def chunk_step(c, carry):
        peak, totals, summed = carry
        span = pl.ds(pl.multiple_of(c * CHUNK, CHUNK), CHUNK)
        s = qk(q_glob, k_all[span, :])
        top = jnp.maximum(peak, jnp.max(s, axis=1, keepdims=True))
        factor = jnp.exp2((peak - top) * EXP2_SCALE)
        w = jnp.exp2((s - top) * EXP2_SCALE)
        totals = totals * factor + jnp.sum(w, axis=1, keepdims=True)
        summed = summed * factor + pv(w, v_all[span, :])
        return top, totals, summed

    height = 2 * gpd * BLK
    initial = (
        jnp.full((height, 1), -1e30, jnp.float32),
        jnp.zeros((height, 1), jnp.float32),
        jnp.zeros((height, LANES), jnp.float32),
    )
    _, totals, summed = lax.fori_loop(0, ranges * tokens // CHUNK, chunk_step, initial)
    for g in range(gpd):
        part = slice(2 * BLK * g, 2 * BLK * (g + 1))
        where = pl.ds(pl.multiple_of(own_ref[g] * BLK, BLK), BLK)
        out_ref[where, :] = finish(summed[part], totals[part])


def pair_call(pair, rand, win, glob, own, queries, k_parts, v_parts, so_far):
    tokens, columns = queries.shape
    ranges = len(k_parts)
    gpd = own.shape[0]
    smem = pl.BlockSpec(memory_space=pltpu.SMEM)
    hbm = pl.BlockSpec(memory_space=pl.ANY)
    half = pl.BlockSpec((tokens, LANES), lambda i: (0, pair))
    operands = [rand, win, glob, own, queries, *k_parts, *v_parts]
    in_specs = [smem] * 4 + [half] + [hbm] * (2 * ranges)
    aliases = {}
    if so_far is not None:
        aliases = {len(operands): 0}
        operands.append(so_far)
        in_specs.append(hbm)
    keys_all = ranges * tokens
    pairs_done = 2 * tokens * (6 + gpd * ranges) * BLK + 2 * gpd * BLK * keys_all
    return pl.pallas_call(
        functools.partial(pair_kernel, pair, ranges, gpd, tokens),
        grid=(1,),
        in_specs=in_specs,
        out_specs=half,
        out_shape=jax.ShapeDtypeStruct((tokens, columns), jnp.bfloat16),
        input_output_aliases=aliases,
        scratch_shapes=[
            pltpu.VMEM((keys_all, LANES), jnp.bfloat16),
            pltpu.VMEM((keys_all, LANES), jnp.bfloat16),
            pltpu.VMEM((gpd * ranges * BLK, LANES), jnp.bfloat16),
            pltpu.VMEM((gpd * ranges * BLK, LANES), jnp.bfloat16),
            pltpu.SemaphoreType.DMA((2 * ranges,)),
        ],
        compiler_params=pltpu.CompilerParams(vmem_limit_bytes=48 * 1024 * 1024),
        cost_estimate=pl.CostEstimate(
            flops=8 * DH * pairs_done, bytes_accessed=4 * keys_all * LANES, transcendentals=pairs_done
        ),
        name="pair",
    )(*operands)


def exchange(array, step):
    count = lax.axis_size("seq")
    return lax.ppermute(array, "seq", [(i, i ^ step) for i in range(count)])


def gathered(array, steps):
    parts = {0: array}
    for step in steps:
        parts.update({at ^ step: exchange(part, step) for at, part in list(parts.items())})
    return [parts[at] for at in range(len(parts))]


def shards(queries, keys, values, rand_blocks, global_blocks):
    tokens, columns = queries.shape
    blocks = tokens // BLK
    count = lax.axis_size("seq")
    rank = lax.axis_index("seq")
    pairs = columns // LANES
    steps = [1 << i for i in range(count.bit_length() - 1)]

    def place(ids):
        return ((ids // blocks) ^ rank) * blocks + ids % blocks

    k_all, v_all = [], []
    for pair in range(pairs):
        lanes = slice(pair * LANES, (pair + 1) * LANES)
        k_all.append(gathered(keys[:, lanes], steps))
        v_all.append(gathered(values[:, lanes], steps[::-1]))
        k_all[pair][0] = keys
        v_all[pair][0] = values
    glob = place(jnp.concatenate(gathered(global_blocks, steps)))
    own = global_blocks - rank * blocks
    win = place((rank * blocks - 1 + jnp.arange(blocks + 2)) % (count * blocks))
    rand = place(rand_blocks)
    out = None
    for pair in range(pairs):
        mine = rand[:, 2 * pair : 2 * pair + 2].reshape(-1)
        out = pair_call(pair, mine, win, glob, own, queries, k_all[pair], v_all[pair], out)
    return out


def solution(mesh):
    in_specs = (
        P(("batch", "seq"), "head"),
        P(("batch", "seq"), "head"),
        P(("batch", "seq"), "head"),
        P(("batch", "seq"), "head", None),
        P(("batch", "seq")),
    )
    out_specs = P(("batch", "seq"), "head")
    return jax.shard_map(shards, mesh=mesh, in_specs=in_specs, out_specs=out_specs, check_vma=False)
```

```python
import functools

import jax
import jax.numpy as jnp
from jax import lax
from jax.experimental import pallas as pl
from jax.experimental.pallas import tpu as pltpu
from jax.sharding import PartitionSpec as P

DH = 64
BLK = 64
RAND = 3
LANES = 2 * DH
ROWS = 4
CHUNK = 1024
EXP2_SCALE = 0.125 * 1.4426950408889634


def qk(q, k):
    return lax.dot_general(q, k, (((1,), (1,)), ((), ())), preferred_element_type=jnp.float32)


def part_kernel(
    pair, wide, gpd, tokens, shared, late, lists_ref, glob_ref, own_ref, q_ref, *refs
):
    ranges = len(wide)
    k_refs, v_refs, refs = refs[:ranges], refs[ranges : 2 * ranges], refs[2 * ranges :]
    if late:
        state_o_ref, state_l_ref, refs = refs[0], refs[1], refs[2:]
        if pair > 0:
            refs = refs[1:]
        out_ref, k_all, v_all, units, k_glob, v_glob, sems = refs
    else:
        out_ref, out_l_ref, k_all, v_all, units, k_glob, v_glob, sems = refs
    blocks = tokens // BLK
    globs = gpd * ranges
    empty = ranges * blocks

    copies = []
    for j in range(ranges):
        span = pl.ds(j * tokens, tokens)
        lanes = pl.ds(pair * LANES, LANES)
        for side, (source, target) in enumerate(((k_refs[j], k_all), (v_refs[j], v_all))):
            source = source.at[:, lanes] if wide[j] else source
            copies.append(pltpu.make_async_copy(source, target.at[span], sems.at[2 * j + side]))
    for copy in copies:
        copy.start()
    v_all[empty * BLK :, :] = jnp.zeros((BLK, LANES), jnp.bfloat16)
    units[:BLK, :] = jnp.ones((BLK, LANES), jnp.bfloat16)
    units[BLK:, :] = jnp.zeros((BLK, LANES), jnp.bfloat16)
    for copy in copies:
        copy.wait()

    first = lax.broadcasted_iota(jnp.int32, (BLK, LANES), 1) < DH

    def split_heads(q):
        zero = jnp.zeros_like(q)
        return [jnp.where(first, q, zero), jnp.where(first, zero, q)]

    def block(ref, position):
        return ref[pl.ds(pl.multiple_of(position * BLK, BLK), BLK), :]

    def unit(position):
        return block(units, (position == empty).astype(jnp.int32))

    def weighted(p, v, ones):
        return jnp.dot(
            p.astype(jnp.bfloat16), jnp.concatenate([v, ones], axis=1),
            preferred_element_type=jnp.float32,
        )

    def fold(rows):
        return jnp.where(first, rows[:BLK], rows[BLK:])

    def finish(b, target, peak, sums):
        top = fold(jnp.broadcast_to(peak, (2 * BLK, LANES))) * EXP2_SCALE
        o, total = fold(sums[:, :LANES]), fold(sums[:, LANES:])
        where = pl.ds(pl.multiple_of(target * BLK, BLK), BLK)
        if late:
            old_o, old_l = block(state_o_ref, b), block(state_l_ref, b)
            level = jnp.maximum(top, old_l)
            old_factor, factor = jnp.exp2(old_l - level), jnp.exp2(top - level)
            o = (old_o * old_factor + o * factor) / (old_factor + total * factor)
            out_ref[where, :] = o.astype(jnp.bfloat16)
        else:
            out_ref[where, :] = o / total
            out_l_ref[where, :] = top + jnp.log2(total)

    for g in range(globs):
        k_glob[g * BLK : (g + 1) * BLK, :] = block(k_all, glob_ref[g])
        v_glob[g * BLK : (g + 1) * BLK, :] = block(v_all, glob_ref[g])

    slots = shared + 2 * RAND

    def rows_step(step, carry):
        base = step * ROWS
        q_bd, k_lists, v_lists = [], [], []
        for u in range(ROWS):
            at = (base + u) * 2 * slots
            q_bd += split_heads(block(q_ref, base + u))
            k_list, v_list, one_list = [], [], []
            for j in range(shared):
                k_at, v_at = lists_ref[at + j], lists_ref[at + slots + j]
                k_list.append(block(k_all, k_at))
                v_list.append(block(v_all, v_at))
                one_list.append(unit(v_at))
            for j in range(shared, shared + RAND):
                k_a, k_b = lists_ref[at + j], lists_ref[at + RAND + j]
                v_a, v_b = lists_ref[at + slots + j], lists_ref[at + slots + RAND + j]
                k_list.append(jnp.where(first, block(k_all, k_a), block(k_all, k_b)))
                v_list.append(jnp.where(first, block(v_all, v_a), block(v_all, v_b)))
                one_list.append(jnp.where(first, unit(v_a), unit(v_b)))
            k_lists.append(jnp.concatenate(k_list, axis=0))
            v_lists.append((jnp.concatenate(v_list, axis=0), jnp.concatenate(one_list, axis=0)))
        q_bd = jnp.concatenate(q_bd, axis=0)
        parts = [slice(2 * BLK * u, 2 * BLK * (u + 1)) for u in range(ROWS)]
        s_own = jnp.concatenate([qk(q_bd[parts[u]], k_lists[u]) for u in range(ROWS)], axis=0)
        s_glob = qk(q_bd, k_glob[...])
        peak = jnp.maximum(
            jnp.max(s_own, axis=1, keepdims=True), jnp.max(s_glob, axis=1, keepdims=True)
        )
        w_own = jnp.exp2((s_own - peak) * EXP2_SCALE)
        w_glob = jnp.exp2((s_glob - peak) * EXP2_SCALE)
        sums_glob = weighted(w_glob, v_glob[...], jnp.ones((globs * BLK, LANES), jnp.bfloat16))
        for u in range(ROWS):
            sums = sums_glob[parts[u]] + weighted(w_own[parts[u]], *v_lists[u])
            finish(base + u, base + u, peak[parts[u]], sums)
        return carry

    lax.fori_loop(0, blocks // ROWS, rows_step, 0)

    q_glob = []
    for g in range(gpd):
        q_glob += split_heads(block(q_ref, own_ref[g]))
    q_glob = jnp.concatenate(q_glob, axis=0)
    chunk_ones = jnp.ones((CHUNK, LANES), jnp.bfloat16)

    def chunk_step(c, carry):
        peak, sums = carry
        span = pl.ds(pl.multiple_of(c * CHUNK, CHUNK), CHUNK)
        s = qk(q_glob, k_all[span, :])
        top = jnp.maximum(peak, jnp.max(s, axis=1, keepdims=True))
        w = jnp.exp2((s - top) * EXP2_SCALE)
        sums = sums * jnp.exp2((peak - top) * EXP2_SCALE) + weighted(w, v_all[span, :], chunk_ones)
        return top, sums

    height = 2 * gpd * BLK
    initial = (
        jnp.full((height, 1), -1e30, jnp.float32),
        jnp.zeros((height, 2 * LANES), jnp.float32),
    )
    peak, sums = lax.fori_loop(0, ranges * tokens // CHUNK, chunk_step, initial)
    for g in range(gpd):
        part = slice(2 * BLK * g, 2 * BLK * (g + 1))
        finish(blocks + g, own_ref[g] if late else blocks + g, peak[part], sums[part])


def part_call(pair, shared, lists, glob, own, queries, k_parts, v_parts, state=None, so_far=None):
    tokens, columns = queries.shape
    ranges = len(k_parts)
    gpd = own.shape[0]
    late = state is not None
    smem = pl.BlockSpec(memory_space=pltpu.SMEM)
    hbm = pl.BlockSpec(memory_space=pl.ANY)
    half = pl.BlockSpec((tokens, LANES), lambda i: (0, pair))
    state_rows = tokens + gpd * BLK
    full = pl.BlockSpec((state_rows, LANES), lambda i: (0, 0))
    operands = [lists, glob, own, queries, *k_parts, *v_parts]
    in_specs = [smem] * 3 + [half] + [hbm] * (2 * ranges)
    aliases = {}
    if late:
        operands += state
        in_specs += [full, full]
        out_specs = half
        out_shape = jax.ShapeDtypeStruct((tokens, columns), jnp.bfloat16)
        if so_far is not None:
            aliases = {len(operands): 0}
            operands.append(so_far)
            in_specs.append(hbm)
    else:
        out_specs = [full, full]
        out_shape = [jax.ShapeDtypeStruct((state_rows, LANES), jnp.float32)] * 2
    keys_all = ranges * tokens
    globs = gpd * ranges * BLK
    listed = (shared + RAND) * BLK
    pairs_done = 2 * tokens * (listed + globs) + 2 * gpd * BLK * keys_all
    wide = tuple(part.shape[1] > LANES for part in k_parts)
    return pl.pallas_call(
        functools.partial(part_kernel, pair, wide, gpd, tokens, shared, late),
        grid=(1,),
        in_specs=in_specs,
        out_specs=out_specs,
        out_shape=out_shape,
        input_output_aliases=aliases,
        scratch_shapes=[
            pltpu.VMEM((keys_all, LANES), jnp.bfloat16),
            pltpu.VMEM((keys_all + BLK, LANES), jnp.bfloat16),
            pltpu.VMEM((2 * BLK, LANES), jnp.bfloat16),
            pltpu.VMEM((globs, LANES), jnp.bfloat16),
            pltpu.VMEM((globs, LANES), jnp.bfloat16),
            pltpu.SemaphoreType.DMA((2 * ranges,)),
        ],
        compiler_params=pltpu.CompilerParams(vmem_limit_bytes=48 * 1024 * 1024),
        cost_estimate=pl.CostEstimate(
            flops=16 * DH * pairs_done,
            bytes_accessed=4 * keys_all * LANES,
            transcendentals=pairs_done,
        ),
        name="late" if late else "early",
    )(*operands)


def exchange(array, step):
    count = lax.axis_size("seq")
    return lax.ppermute(array, "seq", [(i, i ^ step) for i in range(count)])


def gathered(array, steps):
    parts = {0: array}
    last = (1 << len(steps)) - 1
    for step in steps:
        for at, part in list(parts.items()):
            if at ^ step != last:
                parts[at ^ step] = exchange(part, step)
    return [parts[at] for at in range(last)], parts[last ^ steps[-1]]


def shards(queries, keys, values, rand_blocks, global_blocks):
    tokens, columns = queries.shape
    blocks = tokens // BLK
    gpd = global_blocks.shape[0]
    count = lax.axis_size("seq")
    rank = lax.axis_index("seq")
    pairs = columns // LANES
    steps = [1 << i for i in range(count.bit_length() - 1)]
    back = steps[::-1]
    early = count - 1

    k_early, k_send = gathered(keys, steps)
    v_early, v_send = gathered(values, back)
    g_early, g_send = gathered(global_blocks, steps)
    glob = jnp.concatenate(g_early + [exchange(g_send, steps[-1])])
    own = global_blocks - rank * blocks
    k_late, v_late = [], []
    for pair in range(pairs):
        lanes = slice(pair * LANES, (pair + 1) * LANES)
        k_late.append(exchange(k_send[:, lanes], steps[-1]))
        v_late.append(exchange(v_send[:, lanes], back[-1]))

    def place(ids):
        return ((ids // blocks) ^ rank) * blocks + ids % blocks

    glob = place(glob)
    row = jnp.arange(blocks)[:, None]
    window = place((rank * blocks + row + jnp.arange(-1, 2)) % (count * blocks))
    rand = place(rand_blocks)
    glob_early, glob_late = glob[: gpd * early], glob[gpd * early :] - early * blocks
    own_row = jnp.broadcast_to(row, window.shape)
    window_early = window < early * blocks
    window_k = jnp.where(window_early, window, own_row)
    window_v = jnp.where(window_early, window, early * blocks)
    halo = jnp.where(row == 0, window[:, :1], window[:, 2:])
    halo_late = halo >= early * blocks
    halo_k = jnp.where(halo_late, halo - early * blocks, glob_late[0])
    halo_v = jnp.where(halo_late, halo - early * blocks, blocks)

    early_state, out = [], None
    for pair in range(pairs):
        mine = rand[:, 2 * pair : 2 * pair + 2].reshape(blocks, 2 * RAND)
        in_early = mine < early * blocks
        lists = jnp.concatenate(
            [window_k, jnp.where(in_early, mine, row), window_v, jnp.where(in_early, mine, early * blocks)],
            axis=1,
        ).reshape(-1)
        early_state.append(
            part_call(pair, 3, lists, glob_early, own, queries, k_early, v_early)
        )
    for pair in range(pairs):
        mine = rand[:, 2 * pair : 2 * pair + 2].reshape(blocks, 2 * RAND)
        in_late = mine >= early * blocks
        lists = jnp.concatenate(
            [
                halo_k,
                jnp.where(in_late, mine - early * blocks, glob_late[0]),
                halo_v,
                jnp.where(in_late, mine - early * blocks, blocks),
            ],
            axis=1,
        ).reshape(-1)
        out = part_call(
            pair, 1, lists, glob_late, own, queries, [k_late[pair]], [v_late[pair]],
            early_state[pair], out,
        )
    return out


def solution(mesh):
    in_specs = (
        P(("batch", "seq"), "head"),
        P(("batch", "seq"), "head"),
        P(("batch", "seq"), "head"),
        P(("batch", "seq"), "head", None),
        P(("batch", "seq")),
    )
    out_specs = P(("batch", "seq"), "head")
    return jax.shard_map(shards, mesh=mesh, in_specs=in_specs, out_specs=out_specs, check_vma=False)
```

```python
import functools

import jax
import jax.numpy as jnp
from jax import lax
from jax.experimental import pallas as pl
from jax.experimental.pallas import tpu as pltpu
from jax.sharding import PartitionSpec as P

DH = 64
BLK = 64
RAND = 3
LANES = 2 * DH
ROWS = 8
CHUNK = 2048
VMEM_BYTES = 16 * 1024 * 1024
EXP2_SCALE = 0.125 * 1.4426950408889634


def qk(q, k):
    return lax.dot_general(q, k, (((1,), (1,)), ((), ())), preferred_element_type=jnp.float32)


def part_kernel(
    pair, kind, wide, gpd, tokens, shared, lists_ref, flags_ref, glob_ref, own_ref, q_ref, *refs
):
    ranges = len(wide)
    blocks = tokens // BLK
    globs = gpd * ranges
    k_parts, v_parts, refs = refs[:ranges], refs[ranges : 2 * ranges], refs[2 * ranges :]
    if kind == "late":
        state_o_ref, state_l_ref = refs[:2]
        out_ref, k_glob, v_glob = refs[3:] if pair > 0 else refs[2:]
        k_all, v_all = k_parts[0], v_parts[0]
    else:
        if kind == "early":
            out_l_ref, refs = refs[1], refs[:1] + refs[2:]
        elif pair > 0:
            refs = refs[1:]
        out_ref, k_glob, v_glob, k_all, v_all, sems = refs
        copies = []
        for j in range(ranges):
            span = pl.ds(j * tokens, tokens)
            lanes = pl.ds(pair * LANES, LANES)
            for side, (source, target) in enumerate(((k_parts[j], k_all), (v_parts[j], v_all))):
                source = source.at[:, lanes] if wide[j][side] else source
                copies.append(pltpu.make_async_copy(source, target.at[span], sems.at[2 * j + side]))
        for copy in copies:
            copy.start()
        for copy in copies:
            copy.wait()

    first = lax.broadcasted_iota(jnp.int32, (BLK, LANES), 1) < DH
    first_few = lax.broadcasted_iota(jnp.int32, (16, LANES), 1) < DH
    block_ones = jnp.ones((BLK, LANES), jnp.bfloat16)

    def split_heads(q):
        zero = jnp.zeros_like(q)
        return [jnp.where(first, q, zero), jnp.where(first, zero, q)]

    def block(ref, position):
        return ref[pl.ds(pl.multiple_of(position * BLK, BLK), BLK), :]

    def listed(flag_a, flag_b):
        few = jnp.where(first_few, flag_a, flag_b).astype(jnp.bfloat16)
        return jnp.concatenate([few] * (BLK // 16), axis=0)

    def weighted(p, v, ones):
        return jnp.dot(
            p.astype(jnp.bfloat16), jnp.concatenate([v, ones], axis=1),
            preferred_element_type=jnp.float32,
        )

    def fold(rows):
        return jnp.where(first, rows[:BLK], rows[BLK:])

    def finish(b, target, peak, sums):
        o, total = fold(sums[:, :LANES]), fold(sums[:, LANES:])
        where = pl.ds(pl.multiple_of(target * BLK, BLK), BLK)
        if kind == "full":
            out_ref[where, :] = (o / total).astype(jnp.bfloat16)
            return
        top = fold(jnp.broadcast_to(peak, (2 * BLK, LANES))) * EXP2_SCALE
        if kind == "late":
            old_o, old_l = block(state_o_ref, b), block(state_l_ref, b)
            level = jnp.maximum(top, old_l)
            old_factor, factor = jnp.exp2(old_l - level), jnp.exp2(top - level)
            o = (old_o * old_factor + o * factor) / (old_factor + total * factor)
            out_ref[where, :] = o.astype(jnp.bfloat16)
        else:
            out_ref[where, :] = o / total
            out_l_ref[where, :] = top + jnp.log2(total)

    for g in range(globs):
        k_glob[g * BLK : (g + 1) * BLK, :] = block(k_all, glob_ref[g])
        v_glob[g * BLK : (g + 1) * BLK, :] = block(v_all, glob_ref[g])

    slots = shared + 2 * RAND

    def rows_step(step, carry):
        base = step * ROWS
        q_bd, k_lists, v_lists = [], [], []
        for u in range(ROWS):
            at = (base + u) * slots
            q_bd += split_heads(block(q_ref, base + u))
            k_list, v_list, one_list = [], [], []
            for j in range(shared + RAND):
                a, b = (at + j, at + j) if j < shared else (at + j, at + RAND + j)
                k, v = block(k_all, lists_ref[a]), block(v_all, lists_ref[a])
                if j >= shared:
                    k = jnp.where(first, k, block(k_all, lists_ref[b]))
                    v = jnp.where(first, v, block(v_all, lists_ref[b]))
                if kind == "full" or (kind == "early" and j == 1):
                    ones = block_ones
                else:
                    ones = listed(flags_ref[a], flags_ref[b])
                    v = v * ones
                k_list.append(k)
                v_list.append(v)
                one_list.append(ones)
            k_lists.append(jnp.concatenate(k_list, axis=0))
            v_lists.append((jnp.concatenate(v_list, axis=0), jnp.concatenate(one_list, axis=0)))
        q_bd = jnp.concatenate(q_bd, axis=0)
        parts = [slice(2 * BLK * u, 2 * BLK * (u + 1)) for u in range(ROWS)]
        s_own = jnp.concatenate([qk(q_bd[parts[u]], k_lists[u]) for u in range(ROWS)], axis=0)
        s_glob = qk(q_bd, k_glob[...])
        peak = jnp.maximum(
            jnp.max(s_own, axis=1, keepdims=True), jnp.max(s_glob, axis=1, keepdims=True)
        )
        w_own = jnp.exp2((s_own - peak) * EXP2_SCALE)
        w_glob = jnp.exp2((s_glob - peak) * EXP2_SCALE)
        sums_glob = weighted(w_glob, v_glob[...], jnp.ones((globs * BLK, LANES), jnp.bfloat16))
        for u in range(ROWS):
            sums = sums_glob[parts[u]] + weighted(w_own[parts[u]], *v_lists[u])
            finish(base + u, base + u, peak[parts[u]], sums)
        return carry

    lax.fori_loop(0, blocks // ROWS, rows_step, 0)

    q_glob = []
    for g in range(gpd):
        q_glob += split_heads(block(q_ref, own_ref[g]))
    q_glob = jnp.concatenate(q_glob, axis=0)
    chunk_ones = jnp.ones((CHUNK, LANES), jnp.bfloat16)

    def chunk_step(c, carry):
        peak, sums = carry
        span = pl.ds(pl.multiple_of(c * CHUNK, CHUNK), CHUNK)
        s = qk(q_glob, k_all[span, :])
        top = jnp.maximum(peak, jnp.max(s, axis=1, keepdims=True))
        w = jnp.exp2((s - top) * EXP2_SCALE)
        sums = sums * jnp.exp2((peak - top) * EXP2_SCALE) + weighted(w, v_all[span, :], chunk_ones)
        return top, sums

    height = 2 * gpd * BLK
    initial = (
        jnp.full((height, 1), -1e30, jnp.float32),
        jnp.zeros((height, 2 * LANES), jnp.float32),
    )
    peak, sums = lax.fori_loop(0, ranges * tokens // CHUNK, chunk_step, initial)
    for g in range(gpd):
        part = slice(2 * BLK * g, 2 * BLK * (g + 1))
        target = blocks + g if kind == "early" else own_ref[g]
        finish(blocks + g, target, peak[part], sums[part])


def part_call(
    pair, kind, shared, lists, flags, glob, own, queries, k_parts, v_parts, state=(), so_far=None
):
    tokens, columns = queries.shape
    ranges = len(k_parts)
    gpd = own.shape[0]
    smem = pl.BlockSpec(memory_space=pltpu.SMEM)
    hbm = pl.BlockSpec(memory_space=pl.ANY)
    half = pl.BlockSpec((tokens, LANES), lambda i: (0, pair))
    state_rows = tokens + gpd * BLK

    def full(rows):
        return pl.BlockSpec((rows, LANES), lambda i: (0, 0))

    operands = [lists, flags, glob, own, queries, *k_parts, *v_parts, *state]
    in_specs = [smem] * 4 + [half] + [full(tokens) if kind == "late" else hbm] * (2 * ranges)
    in_specs += [full(state_rows)] * len(state)
    aliases = {}
    if so_far is not None:
        aliases = {len(operands): 0}
        operands.append(so_far)
        in_specs.append(hbm)
    if kind == "early":
        out_specs = [full(state_rows)] * 2
        out_shape = [jax.ShapeDtypeStruct((state_rows, LANES), jnp.float32)] * 2
    else:
        out_specs = half
        out_shape = jax.ShapeDtypeStruct((tokens, columns), jnp.bfloat16)
    keys_all = ranges * tokens
    globs = gpd * ranges * BLK
    pairs_done = 2 * tokens * ((shared + RAND) * BLK + globs) + 2 * gpd * BLK * keys_all
    wide = tuple((k.shape[1] > LANES, v.shape[1] > LANES) for k, v in zip(k_parts, v_parts))
    scratch = [pltpu.VMEM((globs, LANES), jnp.bfloat16)] * 2
    if kind != "late":
        scratch += [pltpu.VMEM((keys_all, LANES), jnp.bfloat16)] * 2
        scratch.append(pltpu.SemaphoreType.DMA((2 * ranges,)))
    return pl.pallas_call(
        functools.partial(part_kernel, pair, kind, wide, gpd, tokens, shared),
        grid=(1,),
        in_specs=in_specs,
        out_specs=out_specs,
        out_shape=out_shape,
        input_output_aliases=aliases,
        scratch_shapes=scratch,
        compiler_params=pltpu.CompilerParams(vmem_limit_bytes=VMEM_BYTES + 8 * keys_all * LANES),
        cost_estimate=pl.CostEstimate(
            flops=16 * DH * pairs_done,
            bytes_accessed=4 * keys_all * LANES,
            transcendentals=pairs_done,
        ),
        name=kind,
    )(*operands)


def exchange(array, step):
    count = lax.axis_size("seq")
    return lax.ppermute(array, "seq", [(i, i ^ step) for i in range(count)])


def shards(queries, keys, values, rand_blocks, global_blocks):
    tokens, columns = queries.shape
    blocks = tokens // BLK
    gpd = global_blocks.shape[0]
    count = lax.axis_size("seq")
    rank = lax.axis_index("seq")
    pairs = columns // LANES
    steps = [1 << i for i in range(count.bit_length() - 1)]
    last = count - 1

    def place(ids):
        return ((ids // blocks) ^ rank) * blocks + ids % blocks

    row = jnp.arange(blocks)[:, None]
    window = place((rank * blocks + row + jnp.arange(-1, 2)) % (count * blocks))
    rand = place(rand_blocks)
    glob = jnp.concatenate([global_blocks] + [exchange(global_blocks, j) for j in range(1, count)])
    glob = place(glob)

    back = steps[::-1]
    k_first, v_first = exchange(keys, steps[0]), exchange(values, back[0])
    k_held, v_held, rand, window, glob = lax.optimization_barrier((keys, values, rand, window, glob))
    k_sent, v_sent = [], []
    for pair in range(pairs):
        lanes = slice(pair * LANES, (pair + 1) * LANES)
        k_parts = {0: k_held[:, lanes], steps[0]: k_first[:, lanes]}
        v_parts = {0: v_held[:, lanes], back[0]: v_first[:, lanes]}
        done = []
        for k_step, v_step in zip(steps[1:], back[1:]):
            for k_at, v_at in list(zip(k_parts, v_parts)):
                outgoing = (k_parts[k_at], v_parts[v_at])
                if pair > 0 and not done:
                    outgoing = lax.optimization_barrier(outgoing + (k_first, v_first))[:2]
                done.append((exchange(outgoing[0], k_step), exchange(outgoing[1], v_step)))
                k_parts[k_at ^ k_step], v_parts[v_at ^ v_step] = done[-1]
        k_parts.update({0: keys, steps[0]: k_first})
        v_parts.update({0: values, back[0]: v_first})
        k_sent.append([k_parts[at] for at in range(count)])
        v_sent.append([v_parts[at] for at in range(count)])

    own = global_blocks - rank * blocks

    def call(kind, pair, shared, listed, spare, start, stop, state=(), so_far=None):
        mine = rand[:, 2 * pair : 2 * pair + 2].reshape(blocks, 2 * RAND)
        lists = jnp.concatenate([listed, mine], axis=1)
        inside = (lists >= start * blocks) & (lists < stop * blocks)
        lists = jnp.where(inside, lists - start * blocks, spare)
        return part_call(
            pair, kind, shared, lists.reshape(-1), inside.astype(jnp.float32).reshape(-1),
            glob[gpd * start : gpd * stop] - start * blocks, own, queries,
            k_sent[pair][start:stop], v_sent[pair][start:stop], state, so_far,
        )

    out = None
    for pair in range(pairs - 1):
        out = call("full", pair, 3, window, row, 0, count, so_far=out)
    state = call("early", pairs - 1, 3, window, row, 0, last)
    halo = jnp.where(row == 0, window[:, :1], window[:, 2:])
    spare = glob[gpd * last] - last * blocks
    return call("late", pairs - 1, 1, halo, spare, last, count, state=state, so_far=out)


def solution(mesh):
    in_specs = (
        P(("batch", "seq"), "head"),
        P(("batch", "seq"), "head"),
        P(("batch", "seq"), "head"),
        P(("batch", "seq"), "head", None),
        P(("batch", "seq")),
    )
    out_specs = P(("batch", "seq"), "head")
    return jax.shard_map(shards, mesh=mesh, in_specs=in_specs, out_specs=out_specs, check_vma=False)
```

```python
import functools

import jax
import jax.numpy as jnp
from jax import lax
from jax.experimental import pallas as pl
from jax.experimental.pallas import tpu as pltpu
from jax.sharding import PartitionSpec as P

DH = 64
BLK = 64
RAND = 3
LANES = 2 * DH
ROWS = 8
CHUNK = 2048
SUBS = 2
VMEM_BYTES = 16 * 1024 * 1024
EXP2_SCALE = 0.125 * 1.4426950408889634


def qk(q, k):
    return lax.dot_general(q, k, (((1,), (1,)), ((), ())), preferred_element_type=jnp.float32)


def part_kernel(
    pair, kind, wide, gpd, tokens, shared, lists_ref, flags_ref, glob_ref, own_ref, q_ref, *refs
):
    ranges = len(wide)
    blocks = tokens // BLK
    globs = gpd * ranges
    k_parts, v_parts, refs = refs[:ranges], refs[ranges : 2 * ranges], refs[2 * ranges :]
    if kind == "late":
        state_o_ref, state_l_ref = refs[:2]
        out_ref, k_glob, v_glob = refs[3:] if pair > 0 else refs[2:]
        k_all, v_all = k_parts[0], v_parts[0]
    else:
        if kind == "early":
            out_l_ref, refs = refs[1], refs[:1] + refs[2:]
        elif pair > 0:
            refs = refs[1:]
        out_ref, k_glob, v_glob, k_all, v_all, sems = refs
        copies = []
        for j in range(ranges):
            span = pl.ds(j * tokens, tokens)
            lanes = pl.ds(pair * LANES, LANES)
            for side, (source, target) in enumerate(((k_parts[j], k_all), (v_parts[j], v_all))):
                source = source.at[:, lanes] if wide[j][side] else source
                copies.append(pltpu.make_async_copy(source, target.at[span], sems.at[2 * j + side]))
        for copy in copies:
            copy.start()
        for copy in copies:
            copy.wait()

    first = lax.broadcasted_iota(jnp.int32, (BLK, LANES), 1) < DH
    first_few = lax.broadcasted_iota(jnp.int32, (16, LANES), 1) < DH
    block_ones = jnp.ones((BLK, LANES), jnp.bfloat16)

    def split_heads(q):
        zero = jnp.zeros_like(q)
        return [jnp.where(first, q, zero), jnp.where(first, zero, q)]

    def block(ref, position):
        return ref[pl.ds(pl.multiple_of(position * BLK, BLK), BLK), :]

    def listed(flag_a, flag_b):
        few = jnp.where(first_few, flag_a, flag_b).astype(jnp.bfloat16)
        return jnp.concatenate([few] * (BLK // 16), axis=0)

    def weighted(p, v, ones):
        return jnp.dot(
            p.astype(jnp.bfloat16), jnp.concatenate([v, ones], axis=1),
            preferred_element_type=jnp.float32,
        )

    def fold(rows):
        return jnp.where(first, rows[:BLK], rows[BLK:])

    def finish(b, target, peak, sums):
        o, total = fold(sums[:, :LANES]), fold(sums[:, LANES:])
        where = pl.ds(pl.multiple_of(target * BLK, BLK), BLK)
        if kind == "full":
            out_ref[where, :] = (o / total).astype(jnp.bfloat16)
            return
        top = fold(jnp.broadcast_to(peak, (2 * BLK, LANES))) * EXP2_SCALE
        if kind == "late":
            old_o, old_l = block(state_o_ref, b), block(state_l_ref, b)
            level = jnp.maximum(top, old_l)
            old_factor, factor = jnp.exp2(old_l - level), jnp.exp2(top - level)
            o = (old_o * old_factor + o * factor) / (old_factor + total * factor)
            out_ref[where, :] = o.astype(jnp.bfloat16)
        else:
            out_ref[where, :] = o / total
            out_l_ref[where, :] = top + jnp.log2(total)

    for g in range(globs):
        k_glob[g * BLK : (g + 1) * BLK, :] = block(k_all, glob_ref[g])
        v_glob[g * BLK : (g + 1) * BLK, :] = block(v_all, glob_ref[g])

    slots = shared + 2 * RAND

    glob_ones = jnp.ones((globs * BLK, LANES), jnp.bfloat16)

    def scores(row):
        at = row * slots
        q_bd = jnp.concatenate(split_heads(block(q_ref, row)), axis=0)
        k_list, v_list, one_list = [], [], []
        for j in range(shared + RAND):
            a, b = (at + j, at + j) if j < shared else (at + j, at + RAND + j)
            k, v = block(k_all, lists_ref[a]), block(v_all, lists_ref[a])
            if j >= shared:
                k = jnp.where(first, k, block(k_all, lists_ref[b]))
                v = jnp.where(first, v, block(v_all, lists_ref[b]))
            if kind == "full" or (kind == "early" and j == 1):
                ones = block_ones
            else:
                ones = listed(flags_ref[a], flags_ref[b])
                v = v * ones
            k_list.append(k)
            v_list.append(v)
            one_list.append(ones)
        s = qk(q_bd, jnp.concatenate(k_list + [k_glob[...]], axis=0))
        v = jnp.concatenate(v_list + [v_glob[...]], axis=0)
        return s, v, jnp.concatenate(one_list + [glob_ones], axis=0)

    def rows_step(step, carry):
        base = step * ROWS
        ahead = scores(base)
        for u in range(ROWS):
            (s, v, ones), ahead = ahead, scores(base + u + 1) if u + 1 < ROWS else None
            peak = jnp.max(s, axis=1, keepdims=True)
            w = jnp.exp2((s - peak) * EXP2_SCALE)
            finish(base + u, base + u, peak, weighted(w, v, ones))
        return carry

    lax.fori_loop(0, blocks // ROWS, rows_step, 0)

    q_glob = []
    for g in range(gpd):
        q_glob += split_heads(block(q_ref, own_ref[g]))
    q_glob = jnp.concatenate(q_glob, axis=0)
    chunk_ones = jnp.ones((CHUNK // SUBS, LANES), jnp.bfloat16)

    def chunk_step(c, carry):
        peak, sums = carry
        size = CHUNK // SUBS
        spans = [pl.ds(pl.multiple_of(c * CHUNK + i * size, size), size) for i in range(SUBS)]
        ahead = qk(q_glob, k_all[spans[0], :])
        for i in range(SUBS):
            s, ahead = ahead, qk(q_glob, k_all[spans[i + 1], :]) if i + 1 < SUBS else None
            top = jnp.maximum(peak, jnp.max(s, axis=1, keepdims=True))
            w = jnp.exp2((s - top) * EXP2_SCALE)
            factor = jnp.exp2((peak - top) * EXP2_SCALE)
            sums = sums * factor + weighted(w, v_all[spans[i], :], chunk_ones)
            peak = top
        return peak, sums

    height = 2 * gpd * BLK
    initial = (
        jnp.full((height, 1), -1e30, jnp.float32),
        jnp.zeros((height, 2 * LANES), jnp.float32),
    )
    peak, sums = lax.fori_loop(0, ranges * tokens // CHUNK, chunk_step, initial)
    for g in range(gpd):
        part = slice(2 * BLK * g, 2 * BLK * (g + 1))
        target = blocks + g if kind == "early" else own_ref[g]
        finish(blocks + g, target, peak[part], sums[part])


def part_call(
    pair, kind, shared, lists, flags, glob, own, queries, k_parts, v_parts, state=(), so_far=None
):
    tokens, columns = queries.shape
    ranges = len(k_parts)
    gpd = own.shape[0]
    smem = pl.BlockSpec(memory_space=pltpu.SMEM)
    hbm = pl.BlockSpec(memory_space=pl.ANY)
    half = pl.BlockSpec((tokens, LANES), lambda i: (0, pair))
    state_rows = tokens + gpd * BLK

    def full(rows):
        return pl.BlockSpec((rows, LANES), lambda i: (0, 0))

    operands = [lists, flags, glob, own, queries, *k_parts, *v_parts, *state]
    in_specs = [smem] * 4 + [half] + [full(tokens) if kind == "late" else hbm] * (2 * ranges)
    in_specs += [full(state_rows)] * len(state)
    aliases = {}
    if so_far is not None:
        aliases = {len(operands): 0}
        operands.append(so_far)
        in_specs.append(hbm)
    if kind == "early":
        out_specs = [full(state_rows)] * 2
        out_shape = [jax.ShapeDtypeStruct((state_rows, LANES), jnp.float32)] * 2
    else:
        out_specs = half
        out_shape = jax.ShapeDtypeStruct((tokens, columns), jnp.bfloat16)
    keys_all = ranges * tokens
    globs = gpd * ranges * BLK
    pairs_done = 2 * tokens * ((shared + RAND) * BLK + globs) + 2 * gpd * BLK * keys_all
    wide = tuple((k.shape[1] > LANES, v.shape[1] > LANES) for k, v in zip(k_parts, v_parts))
    scratch = [pltpu.VMEM((globs, LANES), jnp.bfloat16)] * 2
    if kind != "late":
        scratch += [pltpu.VMEM((keys_all, LANES), jnp.bfloat16)] * 2
        scratch.append(pltpu.SemaphoreType.DMA((2 * ranges,)))
    return pl.pallas_call(
        functools.partial(part_kernel, pair, kind, wide, gpd, tokens, shared),
        grid=(1,),
        in_specs=in_specs,
        out_specs=out_specs,
        out_shape=out_shape,
        input_output_aliases=aliases,
        scratch_shapes=scratch,
        compiler_params=pltpu.CompilerParams(vmem_limit_bytes=VMEM_BYTES + 8 * keys_all * LANES),
        cost_estimate=pl.CostEstimate(
            flops=16 * DH * pairs_done,
            bytes_accessed=4 * keys_all * LANES,
            transcendentals=pairs_done,
        ),
        name=kind,
    )(*operands)


def exchange(array, step):
    count = lax.axis_size("seq")
    return lax.ppermute(array, "seq", [(i, i ^ step) for i in range(count)])


def shards(queries, keys, values, rand_blocks, global_blocks):
    tokens, columns = queries.shape
    blocks = tokens // BLK
    gpd = global_blocks.shape[0]
    count = lax.axis_size("seq")
    rank = lax.axis_index("seq")
    pairs = columns // LANES
    steps = [1 << i for i in range(count.bit_length() - 1)]
    last = count - 1

    def place(ids):
        return ((ids // blocks) ^ rank) * blocks + ids % blocks

    row = jnp.arange(blocks)[:, None]
    window = place((rank * blocks + row + jnp.arange(-1, 2)) % (count * blocks))
    rand = place(rand_blocks)
    glob = jnp.concatenate([global_blocks] + [exchange(global_blocks, j) for j in range(1, count)])
    glob = place(glob)

    back = steps[::-1]
    k_first, v_first = exchange(keys, steps[0]), exchange(values, back[0])
    k_held, v_held, rand, window, glob = lax.optimization_barrier((keys, values, rand, window, glob))
    k_sent, v_sent = [], []
    for pair in range(pairs):
        lanes = slice(pair * LANES, (pair + 1) * LANES)
        k_parts = {0: k_held[:, lanes], steps[0]: k_first[:, lanes]}
        v_parts = {0: v_held[:, lanes], back[0]: v_first[:, lanes]}
        done = []
        for k_step, v_step in zip(steps[1:], back[1:]):
            for k_at, v_at in list(zip(k_parts, v_parts)):
                outgoing = (k_parts[k_at], v_parts[v_at])
                if pair > 0:
                    gate = before[len(done)] if done else (k_first, v_first)
                    outgoing = lax.optimization_barrier(outgoing + gate)[:2]
                done.append((exchange(outgoing[0], k_step), exchange(outgoing[1], v_step)))
                k_parts[k_at ^ k_step], v_parts[v_at ^ v_step] = done[-1]
        k_parts.update({0: keys, steps[0]: k_first})
        v_parts.update({0: values, back[0]: v_first})
        k_sent.append([k_parts[at] for at in range(count)])
        v_sent.append([v_parts[at] for at in range(count)])
        before = done

    own = global_blocks - rank * blocks

    def call(kind, pair, shared, listed, spare, start, stop, state=(), so_far=None):
        mine = rand[:, 2 * pair : 2 * pair + 2].reshape(blocks, 2 * RAND)
        lists = jnp.concatenate([listed, mine], axis=1)
        inside = (lists >= start * blocks) & (lists < stop * blocks)
        lists = jnp.where(inside, lists - start * blocks, spare)
        return part_call(
            pair, kind, shared, lists.reshape(-1), inside.astype(jnp.float32).reshape(-1),
            glob[gpd * start : gpd * stop] - start * blocks, own, queries,
            k_sent[pair][start:stop], v_sent[pair][start:stop], state, so_far,
        )

    out = None
    for pair in range(pairs - 1):
        out = call("full", pair, 3, window, row, 0, count, so_far=out)
    window = lax.optimization_barrier((window, out))[0]
    state = call("early", pairs - 1, 3, window, row, 0, last)
    halo = jnp.where(row == 0, window[:, :1], window[:, 2:])
    spare = glob[gpd * last] - last * blocks
    return call("late", pairs - 1, 1, halo, spare, last, count, state=state, so_far=out)


def solution(mesh):
    in_specs = (
        P(("batch", "seq"), "head"),
        P(("batch", "seq"), "head"),
        P(("batch", "seq"), "head"),
        P(("batch", "seq"), "head", None),
        P(("batch", "seq")),
    )
    out_specs = P(("batch", "seq"), "head")
    return jax.shard_map(shards, mesh=mesh, in_specs=in_specs, out_specs=out_specs, check_vma=False)
```

```python
import functools

import jax
import jax.numpy as jnp
from jax import lax
from jax.experimental import pallas as pl
from jax.experimental.pallas import tpu as pltpu
from jax.sharding import PartitionSpec as P

DH = 64
BLK = 64
RAND = 3
LANES = 2 * DH
ROWS = 8
CHUNK = 2048
SUBS = 2
VMEM_BYTES = 16 * 1024 * 1024
EXP2_SCALE = 0.125 * 1.4426950408889634


def qk(q, k):
    return lax.dot_general(q, k, (((1,), (1,)), ((), ())), preferred_element_type=jnp.float32)


def part_kernel(
    pair, kind, wide, gpd, tokens, shared, lists_ref, flags_ref, glob_ref, own_ref, q_ref, *refs
):
    ranges = len(wide)
    blocks = tokens // BLK
    globs = gpd * ranges
    k_parts, v_parts, refs = refs[:ranges], refs[ranges : 2 * ranges], refs[2 * ranges :]
    if kind == "late":
        state_o_ref, state_l_ref = refs[:2]
        out_ref, k_glob, v_glob = refs[3:] if pair > 0 else refs[2:]
        k_all, v_all = k_parts[0], v_parts[0]
    else:
        if kind == "early":
            out_l_ref, refs = refs[1], refs[:1] + refs[2:]
        elif pair > 0:
            refs = refs[1:]
        out_ref, k_glob, v_glob, k_all, v_all, sems = refs
        copies = []
        for j in range(ranges):
            span = pl.ds(j * tokens, tokens)
            lanes = pl.ds(pair * LANES, LANES)
            for side, (source, target) in enumerate(((k_parts[j], k_all), (v_parts[j], v_all))):
                source = source.at[:, lanes] if wide[j][side] else source
                copies.append(pltpu.make_async_copy(source, target.at[span], sems.at[2 * j + side]))
        for copy in copies:
            copy.start()
        for copy in copies:
            copy.wait()

    first = lax.broadcasted_iota(jnp.int32, (BLK, LANES), 1) < DH
    first_few = lax.broadcasted_iota(jnp.int32, (16, LANES), 1) < DH
    block_ones = jnp.ones((BLK, LANES), jnp.bfloat16)

    def split_heads(q):
        zero = jnp.zeros_like(q)
        return [jnp.where(first, q, zero), jnp.where(first, zero, q)]

    def block(ref, position):
        return ref[pl.ds(pl.multiple_of(position * BLK, BLK), BLK), :]

    def listed(flag_a, flag_b):
        few = jnp.where(first_few, flag_a, flag_b).astype(jnp.bfloat16)
        return jnp.concatenate([few] * (BLK // 16), axis=0)

    def weighted(p, v, ones):
        return jnp.dot(
            p.astype(jnp.bfloat16), jnp.concatenate([v, ones], axis=1),
            preferred_element_type=jnp.float32,
        )

    def fold(rows):
        return jnp.where(first, rows[:BLK], rows[BLK:])

    def finish(b, target, peak, sums):
        o, total = fold(sums[:, :LANES]), fold(sums[:, LANES:])
        where = pl.ds(pl.multiple_of(target * BLK, BLK), BLK)
        if kind == "full":
            out_ref[where, :] = (o / total).astype(jnp.bfloat16)
            return
        top = fold(jnp.broadcast_to(peak, (2 * BLK, LANES))) * EXP2_SCALE
        if kind == "late":
            old_o, old_l = block(state_o_ref, b), block(state_l_ref, b)
            level = jnp.maximum(top, old_l)
            old_factor, factor = jnp.exp2(old_l - level), jnp.exp2(top - level)
            o = (old_o * old_factor + o * factor) / (old_factor + total * factor)
            out_ref[where, :] = o.astype(jnp.bfloat16)
        else:
            out_ref[where, :] = o / total
            out_l_ref[where, :] = top + jnp.log2(total)

    for g in range(globs):
        k_glob[g * BLK : (g + 1) * BLK, :] = block(k_all, glob_ref[g])
        v_glob[g * BLK : (g + 1) * BLK, :] = block(v_all, glob_ref[g])

    slots = shared + 2 * RAND

    glob_ones = jnp.ones((globs * BLK, LANES), jnp.bfloat16)

    def scores(row):
        at = row * slots
        q_bd = jnp.concatenate(split_heads(block(q_ref, row)), axis=0)
        k_list, v_list, one_list = [], [], []
        for j in range(shared + RAND):
            a, b = (at + j, at + j) if j < shared else (at + j, at + RAND + j)
            k, v = block(k_all, lists_ref[a]), block(v_all, lists_ref[a])
            if j >= shared:
                k = jnp.where(first, k, block(k_all, lists_ref[b]))
                v = jnp.where(first, v, block(v_all, lists_ref[b]))
            if kind == "full" or (kind == "early" and j == 1):
                ones = block_ones
            else:
                ones = listed(flags_ref[a], flags_ref[b])
                v = v * ones
            k_list.append(k)
            v_list.append(v)
            one_list.append(ones)
        s = qk(q_bd, jnp.concatenate(k_list + [k_glob[...]], axis=0))
        v = jnp.concatenate(v_list + [v_glob[...]], axis=0)
        return s, v, jnp.concatenate(one_list + [glob_ones], axis=0)

    def rows_step(step, carry):
        base = step * ROWS
        ahead = scores(base)
        for u in range(ROWS):
            (s, v, ones), ahead = ahead, scores(base + u + 1) if u + 1 < ROWS else None
            peak = jnp.max(s, axis=1, keepdims=True)
            w = jnp.exp2((s - peak) * EXP2_SCALE)
            finish(base + u, base + u, peak, weighted(w, v, ones))
        return carry

    lax.fori_loop(0, blocks // ROWS, rows_step, 0)

    q_glob = []
    for g in range(gpd):
        q_glob += split_heads(block(q_ref, own_ref[g]))
    q_glob = jnp.concatenate(q_glob, axis=0)
    chunk_ones = jnp.ones((CHUNK // SUBS, LANES), jnp.bfloat16)

    def chunk_step(c, carry):
        peak, sums = carry
        size = CHUNK // SUBS
        spans = [pl.ds(pl.multiple_of(c * CHUNK + i * size, size), size) for i in range(SUBS)]
        ahead = qk(q_glob, k_all[spans[0], :])
        for i in range(SUBS):
            s, ahead = ahead, qk(q_glob, k_all[spans[i + 1], :]) if i + 1 < SUBS else None
            top = jnp.maximum(peak, jnp.max(s, axis=1, keepdims=True))
            w = jnp.exp2((s - top) * EXP2_SCALE)
            factor = jnp.exp2((peak - top) * EXP2_SCALE)
            sums = sums * factor + weighted(w, v_all[spans[i], :], chunk_ones)
            peak = top
        return peak, sums

    height = 2 * gpd * BLK
    initial = (
        jnp.full((height, 1), -1e30, jnp.float32),
        jnp.zeros((height, 2 * LANES), jnp.float32),
    )
    peak, sums = lax.fori_loop(0, ranges * tokens // CHUNK, chunk_step, initial)
    for g in range(gpd):
        part = slice(2 * BLK * g, 2 * BLK * (g + 1))
        target = blocks + g if kind == "early" else own_ref[g]
        finish(blocks + g, target, peak[part], sums[part])


def part_call(
    pair, kind, shared, lists, flags, glob, own, queries, k_parts, v_parts, state=(), so_far=None
):
    tokens, columns = queries.shape
    ranges = len(k_parts)
    gpd = own.shape[0]
    smem = pl.BlockSpec(memory_space=pltpu.SMEM)
    hbm = pl.BlockSpec(memory_space=pl.ANY)
    half = pl.BlockSpec((tokens, LANES), lambda i: (0, pair))
    state_rows = tokens + gpd * BLK

    def full(rows):
        return pl.BlockSpec((rows, LANES), lambda i: (0, 0))

    operands = [lists, flags, glob, own, queries, *k_parts, *v_parts, *state]
    in_specs = [smem] * 4 + [half] + [full(tokens) if kind == "late" else hbm] * (2 * ranges)
    in_specs += [full(state_rows)] * len(state)
    aliases = {}
    if so_far is not None:
        aliases = {len(operands): 0}
        operands.append(so_far)
        in_specs.append(hbm)
    if kind == "early":
        out_specs = [full(state_rows)] * 2
        out_shape = [jax.ShapeDtypeStruct((state_rows, LANES), jnp.float32)] * 2
    else:
        out_specs = half
        out_shape = jax.ShapeDtypeStruct((tokens, columns), jnp.bfloat16)
    keys_all = ranges * tokens
    globs = gpd * ranges * BLK
    pairs_done = 2 * tokens * ((shared + RAND) * BLK + globs) + 2 * gpd * BLK * keys_all
    wide = tuple((k.shape[1] > LANES, v.shape[1] > LANES) for k, v in zip(k_parts, v_parts))
    scratch = [pltpu.VMEM((globs, LANES), jnp.bfloat16)] * 2
    if kind != "late":
        scratch += [pltpu.VMEM((keys_all, LANES), jnp.bfloat16)] * 2
        scratch.append(pltpu.SemaphoreType.DMA((2 * ranges,)))
    return pl.pallas_call(
        functools.partial(part_kernel, pair, kind, wide, gpd, tokens, shared),
        grid=(1,),
        in_specs=in_specs,
        out_specs=out_specs,
        out_shape=out_shape,
        input_output_aliases=aliases,
        scratch_shapes=scratch,
        compiler_params=pltpu.CompilerParams(vmem_limit_bytes=VMEM_BYTES + 8 * keys_all * LANES),
        cost_estimate=pl.CostEstimate(
            flops=16 * DH * pairs_done,
            bytes_accessed=4 * keys_all * LANES,
            transcendentals=pairs_done,
        ),
        name=kind,
    )(*operands)


def exchange(array, step):
    count = lax.axis_size("seq")
    return lax.ppermute(array, "seq", [(i, i ^ step) for i in range(count)])


def shards(queries, keys, values, rand_blocks, global_blocks):
    tokens, columns = queries.shape
    blocks = tokens // BLK
    gpd = global_blocks.shape[0]
    count = lax.axis_size("seq")
    rank = lax.axis_index("seq")
    pairs = columns // LANES
    steps = [1 << i for i in range(count.bit_length() - 1)]
    last = count - 1

    def place(ids):
        return ((ids // blocks) ^ rank) * blocks + ids % blocks

    row = jnp.arange(blocks)[:, None]
    window = place((rank * blocks + row + jnp.arange(-1, 2)) % (count * blocks))
    rand = place(rand_blocks)

    back = steps[::-1]
    k_first, v_first = exchange(keys, steps[0]), exchange(values, back[0])
    glob = [global_blocks] + [exchange(global_blocks, j) for j in range(1, count)]
    glob = place(jnp.concatenate(glob))
    k_held, v_held, glob, rand, window = lax.optimization_barrier((keys, values, glob, rand, window))
    own = global_blocks - rank * blocks
    halo = jnp.where(row == 0, window[:, :1], window[:, 2:])

    def call(kind, pair, k_parts, v_parts, shared, listed, spare, state=(), so_far=None):
        start, stop = (last, count) if kind == "late" else (0, last)
        mine = rand[:, 2 * pair : 2 * pair + 2].reshape(blocks, 2 * RAND)
        lists = jnp.concatenate([listed, mine], axis=1)
        inside = (lists >= start * blocks) & (lists < stop * blocks)
        lists = jnp.where(inside, lists - start * blocks, spare)
        return part_call(
            pair, kind, shared, lists.reshape(-1), inside.astype(jnp.float32).reshape(-1),
            glob[gpd * start : gpd * stop] - start * blocks, own, queries,
            [k_parts[at] for at in range(start, stop)], [v_parts[at] for at in range(start, stop)],
            state, so_far,
        )

    out, state = None, None
    for pair in range(pairs):
        lanes = slice(pair * LANES, (pair + 1) * LANES)
        k_parts = {0: k_held[:, lanes], steps[0]: k_first[:, lanes]}
        v_parts = {0: v_held[:, lanes], back[0]: v_first[:, lanes]}
        done = 0
        for k_step, v_step in zip(steps[1:], back[1:]):
            for k_at, v_at in list(zip(k_parts, v_parts)):
                outgoing = (k_parts[k_at], v_parts[v_at])
                if pair > 0:
                    gate = state if done else (k_first, v_first)
                    outgoing = lax.optimization_barrier((*outgoing, *gate))[:2]
                k_parts[k_at ^ k_step] = exchange(outgoing[0], k_step)
                v_parts[v_at ^ v_step] = exchange(outgoing[1], v_step)
                done += 1
        k_parts.update({0: keys, steps[0]: k_first})
        v_parts.update({0: values, back[0]: v_first})
        if pair > 0:
            window = lax.optimization_barrier((window, out))[0]
        state = call("early", pair, k_parts, v_parts, 3, window, row)
        spare = glob[gpd * last] - last * blocks
        out = call("late", pair, k_parts, v_parts, 1, halo, spare, state, out)
    return out


def solution(mesh):
    in_specs = (
        P(("batch", "seq"), "head"),
        P(("batch", "seq"), "head"),
        P(("batch", "seq"), "head"),
        P(("batch", "seq"), "head", None),
        P(("batch", "seq")),
    )
    out_specs = P(("batch", "seq"), "head")
    return jax.shard_map(shards, mesh=mesh, in_specs=in_specs, out_specs=out_specs, check_vma=False)
```

```python
import functools

import jax
import jax.numpy as jnp
from jax import lax
from jax.experimental import pallas as pl
from jax.experimental.pallas import tpu as pltpu
from jax.sharding import PartitionSpec as P

DH = 64
BLK = 64
RAND = 3
LANES = 2 * DH
ROWS = 16
ID_ROWS = 16
CHUNK = 2048
SUBS = 2
VMEM_BYTES = 16 * 1024 * 1024
EXP2_SCALE = 0.125 * 1.4426950408889634


def qk(q, k):
    return lax.dot_general(q, k, (((1,), (1,)), ((), ())), preferred_element_type=jnp.float32)


def part_kernel(
    pair, kind, wide, gpd, tokens, shared, lists_ref, flags_ref, glob_ref, own_ref, q_ref, *refs
):
    ranges = len(wide)
    blocks = tokens // BLK
    globs = gpd * ranges
    k_parts, v_parts, refs = refs[:ranges], refs[ranges : 2 * ranges], refs[2 * ranges :]
    if kind == "late":
        state_o_ref, state_l_ref = refs[:2]
        out_ref, k_glob, v_glob = refs[3:] if pair > 0 else refs[2:]
        k_all, v_all = k_parts[0], v_parts[0]
    else:
        if kind == "early":
            out_l_ref, refs = refs[1], refs[:1] + refs[2:]
        elif pair > 0:
            refs = refs[1:]
        out_ref, k_glob, v_glob, k_all, v_all, sems = refs
        copies = []
        for j in range(ranges):
            span = pl.ds(j * tokens, tokens)
            lanes = pl.ds(pair * LANES, LANES)
            for side, (source, target) in enumerate(((k_parts[j], k_all), (v_parts[j], v_all))):
                source = source.at[:tokens, lanes] if wide[j][side] else source.at[:tokens]
                copies.append(pltpu.make_async_copy(source, target.at[span], sems.at[2 * j + side]))
        for copy in copies:
            copy.start()
        for copy in copies:
            copy.wait()

    first = lax.broadcasted_iota(jnp.int32, (BLK, LANES), 1) < DH
    first_few = lax.broadcasted_iota(jnp.int32, (16, LANES), 1) < DH
    block_ones = jnp.ones((BLK, LANES), jnp.bfloat16)

    def split_heads(q):
        zero = jnp.zeros_like(q)
        return [jnp.where(first, q, zero), jnp.where(first, zero, q)]

    def block(ref, position):
        return ref[pl.ds(pl.multiple_of(position * BLK, BLK), BLK), :]

    def listed(flag_a, flag_b):
        few = jnp.where(first_few, flag_a, flag_b).astype(jnp.bfloat16)
        return jnp.concatenate([few] * (BLK // 16), axis=0)

    def weighted(p, v, ones):
        return jnp.dot(
            p.astype(jnp.bfloat16), jnp.concatenate([v, ones], axis=1),
            preferred_element_type=jnp.float32,
        )

    def fold(rows):
        return jnp.where(first, rows[:BLK], rows[BLK:])

    def finish(b, target, peak, sums):
        o, total = fold(sums[:, :LANES]), fold(sums[:, LANES:])
        where = pl.ds(pl.multiple_of(target * BLK, BLK), BLK)
        top = fold(jnp.broadcast_to(peak, (2 * BLK, LANES))) * EXP2_SCALE
        if kind == "late":
            old_o, old_l = block(state_o_ref, b), block(state_l_ref, b)
            level = jnp.maximum(top, old_l)
            old_factor, factor = jnp.exp2(old_l - level), jnp.exp2(top - level)
            o = (old_o * old_factor + o * factor) / (old_factor + total * factor)
            out_ref[where, :] = o.astype(jnp.bfloat16)
        else:
            out_ref[where, :] = o / total
            out_l_ref[where, :] = top + jnp.log2(total)

    for g in range(globs):
        k_glob[g * BLK : (g + 1) * BLK, :] = block(k_all, glob_ref[g])
        v_glob[g * BLK : (g + 1) * BLK, :] = block(v_all, glob_ref[g])

    slots = shared + 2 * RAND

    glob_ones = jnp.ones((globs * BLK, LANES), jnp.bfloat16)

    def scores(row):
        at = row * slots
        q_bd = jnp.concatenate(split_heads(block(q_ref, row)), axis=0)
        k_list, v_list, one_list = [], [], []
        for j in range(shared + RAND):
            a, b = (at + j, at + j) if j < shared else (at + j, at + RAND + j)
            k, v = block(k_all, lists_ref[a]), block(v_all, lists_ref[a])
            if j >= shared:
                k = jnp.where(first, k, block(k_all, lists_ref[b]))
                v = jnp.where(first, v, block(v_all, lists_ref[b]))
            if kind == "early" and j == 1:
                ones = block_ones
            else:
                ones = listed(flags_ref[a], flags_ref[b])
                v = v * ones
            k_list.append(k)
            v_list.append(v)
            one_list.append(ones)
        s = qk(q_bd, jnp.concatenate(k_list + [k_glob[...]], axis=0))
        v = jnp.concatenate(v_list + [v_glob[...]], axis=0)
        return s, v, jnp.concatenate(one_list + [glob_ones], axis=0)

    def rows_step(step, carry):
        base = step * ROWS
        ahead = scores(base)
        for u in range(ROWS):
            (s, v, ones), ahead = ahead, scores(base + u + 1) if u + 1 < ROWS else None
            peak = jnp.max(s, axis=1, keepdims=True)
            w = jnp.exp2((s - peak) * EXP2_SCALE)
            finish(base + u, base + u, peak, weighted(w, v, ones))
        return carry

    lax.fori_loop(0, blocks // ROWS, rows_step, 0)

    q_glob = []
    for g in range(gpd):
        q_glob += split_heads(block(q_ref, own_ref[g]))
    q_glob = jnp.concatenate(q_glob, axis=0)
    chunk_ones = jnp.ones((CHUNK // SUBS, LANES), jnp.bfloat16)

    def chunk_step(c, carry):
        peak, sums = carry
        size = CHUNK // SUBS
        spans = [pl.ds(pl.multiple_of(c * CHUNK + i * size, size), size) for i in range(SUBS)]
        ahead = qk(q_glob, k_all[spans[0], :])
        for i in range(SUBS):
            s, ahead = ahead, qk(q_glob, k_all[spans[i + 1], :]) if i + 1 < SUBS else None
            top = jnp.maximum(peak, jnp.max(s, axis=1, keepdims=True))
            w = jnp.exp2((s - top) * EXP2_SCALE)
            factor = jnp.exp2((peak - top) * EXP2_SCALE)
            sums = sums * factor + weighted(w, v_all[spans[i], :], chunk_ones)
            peak = top
        return peak, sums

    height = 2 * gpd * BLK
    initial = (
        jnp.full((height, 1), -1e30, jnp.float32),
        jnp.zeros((height, 2 * LANES), jnp.float32),
    )
    peak, sums = lax.fori_loop(0, ranges * tokens // CHUNK, chunk_step, initial)
    for g in range(gpd):
        part = slice(2 * BLK * g, 2 * BLK * (g + 1))
        target = blocks + g if kind == "early" else own_ref[g]
        finish(blocks + g, target, peak[part], sums[part])


def part_call(
    pair, kind, shared, lists, flags, glob, own, queries, k_parts, v_parts, state=(), so_far=None
):
    tokens, columns = queries.shape
    ranges = len(k_parts)
    gpd = own.shape[0]
    smem = pl.BlockSpec(memory_space=pltpu.SMEM)
    hbm = pl.BlockSpec(memory_space=pl.ANY)
    half = pl.BlockSpec((tokens, LANES), lambda i: (0, pair))
    state_rows = tokens + gpd * BLK

    def full(rows):
        return pl.BlockSpec((rows, LANES), lambda i: (0, 0))

    operands = [lists, flags, glob, own, queries, *k_parts, *v_parts, *state]
    in_specs = [smem] * 4 + [half] + [full(tokens) if kind == "late" else hbm] * (2 * ranges)
    in_specs += [full(state_rows)] * len(state)
    aliases = {}
    if so_far is not None:
        aliases = {len(operands): 0}
        operands.append(so_far)
        in_specs.append(hbm)
    if kind == "early":
        out_specs = [full(state_rows)] * 2
        out_shape = [jax.ShapeDtypeStruct((state_rows, LANES), jnp.float32)] * 2
    else:
        out_specs = half
        out_shape = jax.ShapeDtypeStruct((tokens, columns), jnp.bfloat16)
    keys_all = ranges * tokens
    globs = gpd * ranges * BLK
    pairs_done = 2 * tokens * ((shared + RAND) * BLK + globs) + 2 * gpd * BLK * keys_all
    wide = tuple((k.shape[1] > LANES, v.shape[1] > LANES) for k, v in zip(k_parts, v_parts))
    scratch = [pltpu.VMEM((globs, LANES), jnp.bfloat16)] * 2
    if kind != "late":
        scratch += [pltpu.VMEM((keys_all, LANES), jnp.bfloat16)] * 2
        scratch.append(pltpu.SemaphoreType.DMA((2 * ranges,)))
    return pl.pallas_call(
        functools.partial(part_kernel, pair, kind, wide, gpd, tokens, shared),
        grid=(1,),
        in_specs=in_specs,
        out_specs=out_specs,
        out_shape=out_shape,
        input_output_aliases=aliases,
        scratch_shapes=scratch,
        compiler_params=pltpu.CompilerParams(vmem_limit_bytes=VMEM_BYTES + 8 * keys_all * LANES),
        cost_estimate=pl.CostEstimate(
            flops=16 * DH * pairs_done,
            bytes_accessed=4 * keys_all * LANES,
            transcendentals=pairs_done,
        ),
        name=kind,
    )(*operands)


def exchange(array, step):
    count = lax.axis_size("seq")
    return lax.ppermute(array, "seq", [(i, i ^ step) for i in range(count)])


def shards(queries, keys, values, rand_blocks, global_blocks):
    tokens, columns = queries.shape
    blocks = tokens // BLK
    gpd = global_blocks.shape[0]
    count = lax.axis_size("seq")
    rank = lax.axis_index("seq")
    pairs = columns // LANES
    steps = [1 << i for i in range(count.bit_length() - 1)]
    last = count - 1

    def place(ids):
        return ((ids // blocks) ^ rank) * blocks + ids % blocks

    row = jnp.arange(blocks)[:, None]
    window = place((rank * blocks + row + jnp.arange(-1, 2)) % (count * blocks))
    rand = place(rand_blocks)

    back = steps[::-1]
    k_first, v_first = exchange(keys, steps[0]), exchange(values, back[0])
    k_held, v_held, own, rand, window = lax.optimization_barrier(
        (keys, values, global_blocks - rank * blocks, rand, window)
    )
    id_rows = jnp.pad(own[None].astype(keys.dtype), ((0, ID_ROWS - 1), (0, LANES - gpd)))
    direct = [at for at in range(count) if at & steps[0] and at & back[0]]
    glob = {at: exchange(own, at) for at in direct}
    halo = jnp.where(row == 0, window[:, :1], window[:, 2:])

    def call(kind, pair, k_parts, v_parts, shared, listed, spare, state=(), so_far=None):
        start, stop = (last, count) if kind == "late" else (0, last)
        mine = rand[:, 2 * pair : 2 * pair + 2].reshape(blocks, 2 * RAND)
        lists = jnp.concatenate([listed, mine], axis=1)
        inside = (lists >= start * blocks) & (lists < stop * blocks)
        lists = jnp.where(inside, lists - start * blocks, spare)
        return part_call(
            pair, kind, shared, lists.reshape(-1), inside.astype(jnp.float32).reshape(-1),
            glob[gpd * start : gpd * stop] - start * blocks, own, queries,
            [k_parts[at] for at in range(start, stop)], [v_parts[at] for at in range(start, stop)],
            state, so_far,
        )

    out, state = None, None
    for pair in range(pairs):
        lanes = slice(pair * LANES, (pair + 1) * LANES)
        k_parts = {0: k_held[:, lanes], steps[0]: k_first[:, lanes]}
        v_parts = {0: v_held[:, lanes], back[0]: v_first[:, lanes]}
        if pair == 0:
            k_parts[0] = jnp.concatenate([k_parts[0], id_rows])
            v_parts[0] = jnp.concatenate([v_parts[0], id_rows])
        done, sent = 0, []
        for k_step, v_step in zip(steps[1:], back[1:]):
            for k_at, v_at in list(zip(k_parts, v_parts)):
                outgoing = (k_parts[k_at], v_parts[v_at])
                if pair > 0:
                    gate = state if done else (k_first, v_first)
                    outgoing = lax.optimization_barrier((*outgoing, *gate))[:2]
                sent += outgoing
                k_parts[k_at ^ k_step] = exchange(outgoing[0], k_step)
                v_parts[v_at ^ v_step] = exchange(outgoing[1], v_step)
                done += 1
        k_parts.update({0: keys, steps[0]: k_first})
        v_parts.update({0: values, back[0]: v_first})
        if pair == 0:
            glob[0] = own
            for at in range(1, count):
                carrier = glob[at] if at in direct else v_parts[at] if at & steps[0] else k_parts[at]
                carrier = lax.optimization_barrier((carrier, *sent))[0]
                glob[at] = carrier if at in direct else carrier[tokens, :gpd].astype(jnp.int32)
            glob = jnp.concatenate([glob[at] + at * blocks for at in range(count)])
        else:
            window = lax.optimization_barrier((window, out))[0]
        state = call("early", pair, k_parts, v_parts, 3, window, row)
        spare = glob[gpd * last] - last * blocks
        out = call("late", pair, k_parts, v_parts, 1, halo, spare, state, out)
    return out


def solution(mesh):
    in_specs = (
        P(("batch", "seq"), "head"),
        P(("batch", "seq"), "head"),
        P(("batch", "seq"), "head"),
        P(("batch", "seq"), "head", None),
        P(("batch", "seq")),
    )
    out_specs = P(("batch", "seq"), "head")
    return jax.shard_map(shards, mesh=mesh, in_specs=in_specs, out_specs=out_specs, check_vma=False)
```

```python
import functools

import jax
import jax.numpy as jnp
from jax import lax
from jax.experimental import pallas as pl
from jax.experimental.pallas import tpu as pltpu
from jax.sharding import PartitionSpec as P

DH = 64
BLK = 64
RAND = 3
LANES = 2 * DH
ROWS = 16
ID_ROWS = 16
CHUNK = 2048
SUBS = 2
VMEM_BYTES = 16 * 1024 * 1024
EXP2_SCALE = 0.125 * 1.4426950408889634


def qk(q, k):
    return lax.dot_general(q, k, (((1,), (1,)), ((), ())), preferred_element_type=jnp.float32)


def part_kernel(
    pair, kind, wide, gpd, tokens, shared, lists_ref, flags_ref, glob_ref, own_ref, q_ref, *refs
):
    ranges = len(wide)
    blocks = tokens // BLK
    globs = gpd * ranges
    k_parts, v_parts, refs = refs[:ranges], refs[ranges : 2 * ranges], refs[2 * ranges :]
    if kind == "late":
        state_o_ref, state_l_ref = refs[:2]
        out_ref, k_glob, v_glob = refs[3:] if pair > 0 else refs[2:]
        k_all, v_all = k_parts[0], v_parts[0]
    else:
        if kind == "early":
            out_l_ref, refs = refs[1], refs[:1] + refs[2:]
        elif pair > 0:
            refs = refs[1:]
        out_ref, k_glob, v_glob, k_all, v_all, sems = refs
        copies = []
        for j in range(ranges):
            span = pl.ds(j * tokens, tokens)
            lanes = pl.ds(pair * LANES, LANES)
            for side, (source, target) in enumerate(((k_parts[j], k_all), (v_parts[j], v_all))):
                source = source.at[:tokens, lanes] if wide[j][side] else source.at[:tokens]
                copies.append(pltpu.make_async_copy(source, target.at[span], sems.at[2 * j + side]))
        for copy in copies:
            copy.start()
        for copy in copies:
            copy.wait()

    first = lax.broadcasted_iota(jnp.int32, (BLK, LANES), 1) < DH
    first_few = lax.broadcasted_iota(jnp.int32, (16, LANES), 1) < DH
    block_ones = jnp.ones((BLK, LANES), jnp.bfloat16)

    def split_heads(q):
        zero = jnp.zeros_like(q)
        return [jnp.where(first, q, zero), jnp.where(first, zero, q)]

    def block(ref, position):
        return ref[pl.ds(pl.multiple_of(position * BLK, BLK), BLK), :]

    def listed(flag_a, flag_b):
        few = jnp.where(first_few, flag_a, flag_b).astype(jnp.bfloat16)
        return jnp.concatenate([few] * (BLK // 16), axis=0)

    def weighted(p, v, ones):
        return jnp.dot(
            p.astype(jnp.bfloat16), jnp.concatenate([v, ones], axis=1),
            preferred_element_type=jnp.float32,
        )

    def fold(rows):
        return jnp.where(first, rows[:BLK], rows[BLK:])

    def finish(b, target, peak, sums):
        o, total = fold(sums[:, :LANES]), fold(sums[:, LANES:])
        where = pl.ds(pl.multiple_of(target * BLK, BLK), BLK)
        top = fold(jnp.broadcast_to(peak, (2 * BLK, LANES))) * EXP2_SCALE
        if kind == "late":
            old_o, old_l = block(state_o_ref, b), block(state_l_ref, b)
            level = jnp.maximum(top, old_l)
            old_factor, factor = jnp.exp2(old_l - level), jnp.exp2(top - level)
            o = (old_o * old_factor + o * factor) / (old_factor + total * factor)
            out_ref[where, :] = o.astype(jnp.bfloat16)
        else:
            out_ref[where, :] = o / total
            out_l_ref[where, :] = top + jnp.log2(total)

    for g in range(globs):
        k_glob[g * BLK : (g + 1) * BLK, :] = block(k_all, glob_ref[g])
        v_glob[g * BLK : (g + 1) * BLK, :] = block(v_all, glob_ref[g])

    slots = shared + 2 * RAND

    glob_ones = jnp.ones((globs * BLK, LANES), jnp.bfloat16)

    def scores(row):
        at = row * slots
        q_bd = jnp.concatenate(split_heads(block(q_ref, row)), axis=0)
        k_list, v_list, one_list = [], [], []
        for j in range(shared + RAND):
            a, b = (at + j, at + j) if j < shared else (at + j, at + RAND + j)
            k, v = block(k_all, lists_ref[a]), block(v_all, lists_ref[a])
            if j >= shared:
                k = jnp.where(first, k, block(k_all, lists_ref[b]))
                v = jnp.where(first, v, block(v_all, lists_ref[b]))
            if kind == "early" and j == 1:
                ones = block_ones
            else:
                ones = listed(flags_ref[a], flags_ref[b])
                v = v * ones
            k_list.append(k)
            v_list.append(v)
            one_list.append(ones)
        s = qk(q_bd, jnp.concatenate(k_list + [k_glob[...]], axis=0))
        v = jnp.concatenate(v_list + [v_glob[...]], axis=0)
        return s, v, jnp.concatenate(one_list + [glob_ones], axis=0)

    size = blocks if kind == "late" else ROWS

    def rows_step(step, carry):
        base = step * size
        ahead = scores(base)
        for u in range(size):
            (s, v, ones), ahead = ahead, scores(base + u + 1) if u + 1 < size else None
            peak = jnp.max(s, axis=1, keepdims=True)
            w = jnp.exp2((s - peak) * EXP2_SCALE)
            finish(base + u, base + u, peak, weighted(w, v, ones))
        return carry

    rows_step(0, 0) if kind == "late" else lax.fori_loop(0, blocks // ROWS, rows_step, 0)

    q_glob = []
    for g in range(gpd):
        q_glob += split_heads(block(q_ref, own_ref[g]))
    q_glob = jnp.concatenate(q_glob, axis=0)
    chunk_ones = jnp.ones((CHUNK // SUBS, LANES), jnp.bfloat16)

    def chunk_step(c, carry):
        peak, sums = carry
        size = CHUNK // SUBS
        spans = [pl.ds(pl.multiple_of(c * CHUNK + i * size, size), size) for i in range(SUBS)]
        ahead = qk(q_glob, k_all[spans[0], :])
        for i in range(SUBS):
            s, ahead = ahead, qk(q_glob, k_all[spans[i + 1], :]) if i + 1 < SUBS else None
            top = jnp.maximum(peak, jnp.max(s, axis=1, keepdims=True))
            w = jnp.exp2((s - top) * EXP2_SCALE)
            factor = jnp.exp2((peak - top) * EXP2_SCALE)
            sums = sums * factor + weighted(w, v_all[spans[i], :], chunk_ones)
            peak = top
        return peak, sums

    height = 2 * gpd * BLK
    initial = (
        jnp.full((height, 1), -1e30, jnp.float32),
        jnp.zeros((height, 2 * LANES), jnp.float32),
    )
    peak, sums = lax.fori_loop(0, ranges * tokens // CHUNK, chunk_step, initial)
    for g in range(gpd):
        part = slice(2 * BLK * g, 2 * BLK * (g + 1))
        target = blocks + g if kind == "early" else own_ref[g]
        finish(blocks + g, target, peak[part], sums[part])


def part_call(
    pair, kind, shared, lists, flags, glob, own, queries, k_parts, v_parts, state=(), so_far=None
):
    tokens, columns = queries.shape
    ranges = len(k_parts)
    gpd = own.shape[0]
    smem = pl.BlockSpec(memory_space=pltpu.SMEM)
    hbm = pl.BlockSpec(memory_space=pl.ANY)
    half = pl.BlockSpec((tokens, LANES), lambda i: (0, pair))
    state_rows = tokens + gpd * BLK

    def full(rows):
        return pl.BlockSpec((rows, LANES), lambda i: (0, 0))

    operands = [lists, flags, glob, own, queries, *k_parts, *v_parts, *state]
    in_specs = [smem] * 4 + [half] + [full(tokens) if kind == "late" else hbm] * (2 * ranges)
    in_specs += [full(state_rows)] * len(state)
    aliases = {}
    if so_far is not None:
        aliases = {len(operands): 0}
        operands.append(so_far)
        in_specs.append(hbm)
    if kind == "early":
        out_specs = [full(state_rows)] * 2
        out_shape = [jax.ShapeDtypeStruct((state_rows, LANES), jnp.float32)] * 2
    else:
        out_specs = half
        out_shape = jax.ShapeDtypeStruct((tokens, columns), jnp.bfloat16)
    keys_all = ranges * tokens
    globs = gpd * ranges * BLK
    pairs_done = 2 * tokens * ((shared + RAND) * BLK + globs) + 2 * gpd * BLK * keys_all
    wide = tuple((k.shape[1] > LANES, v.shape[1] > LANES) for k, v in zip(k_parts, v_parts))
    scratch = [pltpu.VMEM((globs, LANES), jnp.bfloat16)] * 2
    if kind != "late":
        scratch += [pltpu.VMEM((keys_all, LANES), jnp.bfloat16)] * 2
        scratch.append(pltpu.SemaphoreType.DMA((2 * ranges,)))
    return pl.pallas_call(
        functools.partial(part_kernel, pair, kind, wide, gpd, tokens, shared),
        grid=(1,),
        in_specs=in_specs,
        out_specs=out_specs,
        out_shape=out_shape,
        input_output_aliases=aliases,
        scratch_shapes=scratch,
        compiler_params=pltpu.CompilerParams(vmem_limit_bytes=VMEM_BYTES + 8 * keys_all * LANES),
        cost_estimate=pl.CostEstimate(
            flops=16 * DH * pairs_done,
            bytes_accessed=4 * keys_all * LANES,
            transcendentals=pairs_done,
        ),
        name=kind,
    )(*operands)


def exchange(array, step):
    count = lax.axis_size("seq")
    return lax.ppermute(array, "seq", [(i, i ^ step) for i in range(count)])


def shards(queries, keys, values, rand_blocks, global_blocks):
    tokens, columns = queries.shape
    blocks = tokens // BLK
    gpd = global_blocks.shape[0]
    count = lax.axis_size("seq")
    rank = lax.axis_index("seq")
    pairs = columns // LANES
    steps = [1 << i for i in range(count.bit_length() - 1)]
    last = count - 1

    def place(ids):
        return ((ids // blocks) ^ rank) * blocks + ids % blocks

    row = jnp.arange(blocks)[:, None]
    window = place((rank * blocks + row + jnp.arange(-1, 2)) % (count * blocks))
    rand = place(rand_blocks)

    back = steps[::-1]
    k_first, v_first = exchange(keys, steps[0]), exchange(values, back[0])
    k_held, v_held, own, rand, window = lax.optimization_barrier(
        (keys, values, global_blocks - rank * blocks, rand, window)
    )
    id_rows = jnp.pad(own[None].astype(keys.dtype), ((0, ID_ROWS - 1), (0, LANES - gpd)))
    direct = [at for at in range(count) if at & steps[0] and at & back[0]]
    glob = {at: exchange(own, at) for at in direct}
    halo = jnp.where(row == 0, window[:, :1], window[:, 2:])

    def call(kind, pair, k_parts, v_parts, shared, listed, spare, state=(), so_far=None):
        start, stop = (last, count) if kind == "late" else (0, last)
        mine = rand[:, 2 * pair : 2 * pair + 2].reshape(blocks, 2 * RAND)
        lists = jnp.concatenate([listed, mine], axis=1)
        inside = (lists >= start * blocks) & (lists < stop * blocks)
        lists = jnp.where(inside, lists - start * blocks, spare)
        return part_call(
            pair, kind, shared, lists.reshape(-1), inside.astype(jnp.float32).reshape(-1),
            glob[gpd * start : gpd * stop] - start * blocks, own, queries,
            [k_parts[at] for at in range(start, stop)], [v_parts[at] for at in range(start, stop)],
            state, so_far,
        )

    out, state = None, None
    for pair in range(pairs):
        lanes = slice(pair * LANES, (pair + 1) * LANES)
        k_parts = {0: k_held[:, lanes], steps[0]: k_first[:, lanes]}
        v_parts = {0: v_held[:, lanes], back[0]: v_first[:, lanes]}
        if pair == 0:
            k_parts[0] = jnp.concatenate([k_parts[0], id_rows])
            v_parts[0] = jnp.concatenate([v_parts[0], id_rows])
        done, sent = 0, []
        for k_step, v_step in zip(steps[1:], back[1:]):
            for k_at, v_at in list(zip(k_parts, v_parts)):
                outgoing = (k_parts[k_at], v_parts[v_at])
                if pair > 0:
                    gate = state if done else (k_first, v_first)
                    outgoing = lax.optimization_barrier((*outgoing, *gate))[:2]
                sent += outgoing
                k_parts[k_at ^ k_step] = exchange(outgoing[0], k_step)
                v_parts[v_at ^ v_step] = exchange(outgoing[1], v_step)
                done += 1
        k_parts.update({0: keys, steps[0]: k_first})
        v_parts.update({0: values, back[0]: v_first})
        if pair == 0:
            glob[0] = own
            for at in range(1, count):
                carrier = glob[at] if at in direct else v_parts[at] if at & steps[0] else k_parts[at]
                carrier = lax.optimization_barrier((carrier, *sent))[0]
                glob[at] = carrier if at in direct else carrier[tokens, :gpd].astype(jnp.int32)
            glob = jnp.concatenate([glob[at] + at * blocks for at in range(count)])
        else:
            window = lax.optimization_barrier((window, out))[0]
        state = call("early", pair, k_parts, v_parts, 3, window, row)
        spare = glob[gpd * last] - last * blocks
        out = call("late", pair, k_parts, v_parts, 1, halo, spare, state, out)
    return out


def solution(mesh):
    in_specs = (
        P(("batch", "seq"), "head"),
        P(("batch", "seq"), "head"),
        P(("batch", "seq"), "head"),
        P(("batch", "seq"), "head", None),
        P(("batch", "seq")),
    )
    out_specs = P(("batch", "seq"), "head")
    return jax.shard_map(shards, mesh=mesh, in_specs=in_specs, out_specs=out_specs, check_vma=False)
```

```python
import functools

import jax
import jax.numpy as jnp
from jax import lax
from jax.experimental import pallas as pl
from jax.experimental.pallas import tpu as pltpu
from jax.sharding import PartitionSpec as P

DH = 64
BLK = 64
RAND = 3
LANES = 2 * DH
ROWS = 16
TOGETHER = 8
ID_ROWS = 16
TOGETHER = 8
CHUNK = 2048
SUBS = 2
VMEM_BYTES = 16 * 1024 * 1024
EXP2_SCALE = 0.125 * 1.4426950408889634


def qk(q, k):
    return lax.dot_general(q, k, (((1,), (1,)), ((), ())), preferred_element_type=jnp.float32)


def part_kernel(
    pair, kind, wide, gpd, tokens, shared, lists_ref, flags_ref, glob_ref, own_ref, q_ref, *refs
):
    ranges = len(wide)
    blocks = tokens // BLK
    globs = gpd * ranges
    k_parts, v_parts, refs = refs[:ranges], refs[ranges : 2 * ranges], refs[2 * ranges :]
    if kind == "late":
        q_all, state_o_ref, state_l_ref = q_ref, *refs[:2]
        out_ref, k_glob, v_glob = refs[3:] if pair > 0 else refs[2:]
        k_all, v_all = k_parts[0], v_parts[0]
    else:
        out_ref, out_l_ref, q_all, k_glob, v_glob, k_all, v_all, sems = refs
        lanes = pl.ds(pair * LANES, LANES)
        copies = [pltpu.make_async_copy(q_ref.at[:, lanes], q_all, sems.at[2 * ranges])]
        for j in range(ranges):
            span = pl.ds(j * tokens, tokens)
            for side, (source, target) in enumerate(((k_parts[j], k_all), (v_parts[j], v_all))):
                source = source.at[:tokens, lanes] if wide[j][side] else source.at[:tokens]
                copies.append(pltpu.make_async_copy(source, target.at[span], sems.at[2 * j + side]))
        for copy in copies:
            copy.start()
        for copy in copies:
            copy.wait()

    first = lax.broadcasted_iota(jnp.int32, (BLK, LANES), 1) < DH
    first_few = lax.broadcasted_iota(jnp.int32, (16, LANES), 1) < DH
    block_ones = jnp.ones((BLK, LANES), jnp.bfloat16)

    def split_heads(q):
        zero = jnp.zeros_like(q)
        return [jnp.where(first, q, zero), jnp.where(first, zero, q)]

    def block(ref, position):
        return ref[pl.ds(pl.multiple_of(position * BLK, BLK), BLK), :]

    def listed(flag_a, flag_b):
        few = jnp.where(first_few, flag_a, flag_b).astype(jnp.bfloat16)
        return jnp.concatenate([few] * (BLK // 16), axis=0)

    def weighted(p, v, ones):
        return jnp.dot(
            p.astype(jnp.bfloat16), jnp.concatenate([v, ones], axis=1),
            preferred_element_type=jnp.float32,
        )

    def fold(rows):
        return jnp.where(first, rows[:BLK], rows[BLK:])

    def finish(b, target, peak, sums):
        o, total = fold(sums[:, :LANES]), fold(sums[:, LANES:])
        where = pl.ds(pl.multiple_of(target * BLK, BLK), BLK)
        top = fold(jnp.broadcast_to(peak, (2 * BLK, LANES))) * EXP2_SCALE
        if kind == "late":
            old_o, old_l = block(state_o_ref, b), block(state_l_ref, b)
            level = jnp.maximum(top, old_l)
            old_factor, factor = jnp.exp2(old_l - level), jnp.exp2(top - level)
            o = (old_o * old_factor + o * factor) / (old_factor + total * factor)
            out_ref[where, :] = o.astype(jnp.bfloat16)
        else:
            out_ref[where, :] = o / total
            out_l_ref[where, :] = top + jnp.log2(total)

    for g in range(globs):
        k_glob[g * BLK : (g + 1) * BLK, :] = block(k_all, glob_ref[g])
        v_glob[g * BLK : (g + 1) * BLK, :] = block(v_all, glob_ref[g])

    slots = shared + 2 * RAND

    glob_ones = jnp.ones((globs * BLK, LANES), jnp.bfloat16)

    def parts_of(row):
        at = row * slots
        q_bd = jnp.concatenate(split_heads(block(q_all, row)), axis=0)
        k_list, v_list, one_list = [], [], []
        for j in range(shared + RAND):
            a, b = (at + j, at + j) if j < shared else (at + j, at + RAND + j)
            k, v = block(k_all, lists_ref[a]), block(v_all, lists_ref[a])
            if j >= shared:
                k = jnp.where(first, k, block(k_all, lists_ref[b]))
                v = jnp.where(first, v, block(v_all, lists_ref[b]))
            if kind == "early" and j == 1:
                ones = block_ones
            else:
                ones = listed(flags_ref[a], flags_ref[b])
                v = v * ones
            k_list.append(k)
            v_list.append(v)
            one_list.append(ones)
        return q_bd, k_list, v_list, one_list

    def joined(arrays):
        return jnp.concatenate(arrays, axis=0)

    def scores(row):
        q_bd, k_list, v_list, one_list = parts_of(row)
        s = qk(q_bd, joined(k_list + [k_glob[...]]))
        return s, joined(v_list + [v_glob[...]]), joined(one_list + [glob_ones])

    def early_rows(step, carry):
        base = step * ROWS
        ahead = scores(base)
        for u in range(ROWS):
            (s, v, ones), ahead = ahead, scores(base + u + 1) if u + 1 < ROWS else None
            peak = jnp.max(s, axis=1, keepdims=True)
            w = jnp.exp2((s - peak) * EXP2_SCALE)
            finish(base + u, base + u, peak, weighted(w, v, ones))
        return carry

    def late_rows(base):
        rows = [parts_of(base + u) for u in range(TOGETHER)]
        s_own = [qk(q_bd, joined(k_list)) for q_bd, k_list, _, _ in rows]
        s_glob = qk(joined([q_bd for q_bd, _, _, _ in rows]), k_glob[...])
        sums, w_glob, peaks = [], [], []
        for u, (_, _, v_list, one_list) in enumerate(rows):
            s_here = s_glob[2 * BLK * u : 2 * BLK * (u + 1)]
            peak = jnp.maximum(
                jnp.max(s_own[u], axis=1, keepdims=True), jnp.max(s_here, axis=1, keepdims=True)
            )
            w = jnp.exp2((s_own[u] - peak) * EXP2_SCALE)
            sums.append(weighted(w, joined(v_list), joined(one_list)))
            w_glob.append(jnp.exp2((s_here - peak) * EXP2_SCALE).astype(jnp.bfloat16))
            peaks.append(peak)
        sums_glob = weighted(joined(w_glob), v_glob[...], glob_ones)
        for u in range(TOGETHER):
            here = sums_glob[2 * BLK * u : 2 * BLK * (u + 1)]
            finish(base + u, base + u, peaks[u], sums[u] + here)

    if kind == "late":
        for base in range(0, blocks, TOGETHER):
            late_rows(base)
    else:
        lax.fori_loop(0, blocks // ROWS, early_rows, 0)

    q_glob = []
    for g in range(gpd):
        q_glob += split_heads(block(q_all, own_ref[g]))
    q_glob = jnp.concatenate(q_glob, axis=0)
    chunk_ones = jnp.ones((CHUNK // SUBS, LANES), jnp.bfloat16)

    def chunk_step(c, carry):
        peak, sums = carry
        size = CHUNK // SUBS
        spans = [pl.ds(pl.multiple_of(c * CHUNK + i * size, size), size) for i in range(SUBS)]
        ahead = qk(q_glob, k_all[spans[0], :])
        for i in range(SUBS):
            s, ahead = ahead, qk(q_glob, k_all[spans[i + 1], :]) if i + 1 < SUBS else None
            top = jnp.maximum(peak, jnp.max(s, axis=1, keepdims=True))
            w = jnp.exp2((s - top) * EXP2_SCALE)
            factor = jnp.exp2((peak - top) * EXP2_SCALE)
            sums = sums * factor + weighted(w, v_all[spans[i], :], chunk_ones)
            peak = top
        return peak, sums

    height = 2 * gpd * BLK
    initial = (
        jnp.full((height, 1), -1e30, jnp.float32),
        jnp.zeros((height, 2 * LANES), jnp.float32),
    )
    peak, sums = lax.fori_loop(0, ranges * tokens // CHUNK, chunk_step, initial)
    for g in range(gpd):
        part = slice(2 * BLK * g, 2 * BLK * (g + 1))
        target = blocks + g if kind == "early" else own_ref[g]
        finish(blocks + g, target, peak[part], sums[part])


def part_call(
    pair, kind, shared, lists, flags, glob, own, queries, k_parts, v_parts, state=(), so_far=None
):
    tokens, columns = queries.shape
    if kind == "late":
        *state, queries = state
    ranges = len(k_parts)
    gpd = own.shape[0]
    smem = pl.BlockSpec(memory_space=pltpu.SMEM)
    hbm = pl.BlockSpec(memory_space=pltpu.HBM)
    half = pl.BlockSpec((tokens, LANES), lambda i: (0, pair))
    state_rows = tokens + gpd * BLK

    def full(rows):
        return pl.BlockSpec((rows, LANES), lambda i: (0, 0))

    operands = [lists, flags, glob, own, queries, *k_parts, *v_parts, *state]
    in_specs = [smem] * 4 + [full(tokens) if kind == "late" else hbm] * (1 + 2 * ranges)
    in_specs += [full(state_rows)] * len(state)
    aliases = {}
    if so_far is not None:
        aliases = {len(operands): 0}
        operands.append(so_far)
        in_specs.append(hbm)
    if kind == "early":
        out_specs = [full(state_rows)] * 2 + [full(tokens)]
        out_shape = [jax.ShapeDtypeStruct((state_rows, LANES), jnp.float32)] * 2
        out_shape.append(jax.ShapeDtypeStruct((tokens, LANES), queries.dtype))
    else:
        out_specs = half
        out_shape = jax.ShapeDtypeStruct((tokens, columns), jnp.bfloat16)
    keys_all = ranges * tokens
    globs = gpd * ranges * BLK
    pairs_done = 2 * tokens * ((shared + RAND) * BLK + globs) + 2 * gpd * BLK * keys_all
    wide = tuple((k.shape[1] > LANES, v.shape[1] > LANES) for k, v in zip(k_parts, v_parts))
    scratch = [pltpu.VMEM((globs, LANES), jnp.bfloat16)] * 2
    if kind != "late":
        scratch += [pltpu.VMEM((keys_all, LANES), jnp.bfloat16)] * 2
        scratch.append(pltpu.SemaphoreType.DMA((2 * ranges + 1,)))
    return pl.pallas_call(
        functools.partial(part_kernel, pair, kind, wide, gpd, tokens, shared),
        grid=(1,),
        in_specs=in_specs,
        out_specs=out_specs,
        out_shape=out_shape,
        input_output_aliases=aliases,
        scratch_shapes=scratch,
        compiler_params=pltpu.CompilerParams(vmem_limit_bytes=VMEM_BYTES + 8 * keys_all * LANES),
        cost_estimate=pl.CostEstimate(
            flops=16 * DH * pairs_done,
            bytes_accessed=4 * keys_all * LANES,
            transcendentals=pairs_done,
        ),
        name=kind,
    )(*operands)


def exchange(array, step):
    count = lax.axis_size("seq")
    return lax.ppermute(array, "seq", [(i, i ^ step) for i in range(count)])


def shards(queries, keys, values, rand_blocks, global_blocks):
    tokens, columns = queries.shape
    blocks = tokens // BLK
    gpd = global_blocks.shape[0]
    count = lax.axis_size("seq")
    rank = lax.axis_index("seq")
    pairs = columns // LANES
    steps = [1 << i for i in range(count.bit_length() - 1)]
    last = count - 1

    def place(ids):
        return ((ids // blocks) ^ rank) * blocks + ids % blocks

    row = jnp.arange(blocks)[:, None]
    window = place((rank * blocks + row + jnp.arange(-1, 2)) % (count * blocks))
    rand = place(rand_blocks)

    back = steps[::-1]
    k_first, v_first = exchange(keys, steps[0]), exchange(values, back[0])
    k_held, v_held, own, rand, window = lax.optimization_barrier(
        (keys, values, global_blocks - rank * blocks, rand, window)
    )
    id_rows = jnp.pad(own[None].astype(keys.dtype), ((0, ID_ROWS - 1), (0, LANES - gpd)))
    direct = [at for at in range(count) if at & steps[0] and at & back[0]]
    glob = {at: exchange(own, at) for at in direct}
    halo = jnp.where(row == 0, window[:, :1], window[:, 2:])

    def call(kind, pair, k_parts, v_parts, shared, listed, spare, state=(), so_far=None):
        start, stop = (last, count) if kind == "late" else (0, last)
        mine = rand[:, 2 * pair : 2 * pair + 2].reshape(blocks, 2 * RAND)
        lists = jnp.concatenate([listed, mine], axis=1)
        inside = (lists >= start * blocks) & (lists < stop * blocks)
        lists = jnp.where(inside, lists - start * blocks, spare)
        return part_call(
            pair, kind, shared, lists.reshape(-1), inside.astype(jnp.float32).reshape(-1),
            glob[gpd * start : gpd * stop] - start * blocks, own, queries,
            [k_parts[at] for at in range(start, stop)], [v_parts[at] for at in range(start, stop)],
            state, so_far,
        )

    out, state = None, None
    for pair in range(pairs):
        lanes = slice(pair * LANES, (pair + 1) * LANES)
        k_parts = {0: k_held[:, lanes], steps[0]: k_first[:, lanes]}
        v_parts = {0: v_held[:, lanes], back[0]: v_first[:, lanes]}
        if pair == 0:
            k_parts[0] = jnp.concatenate([k_parts[0], id_rows])
            v_parts[0] = jnp.concatenate([v_parts[0], id_rows])
        done, sent = 0, []
        for k_step, v_step in zip(steps[1:], back[1:]):
            for k_at, v_at in list(zip(k_parts, v_parts)):
                outgoing = (k_parts[k_at], v_parts[v_at])
                if pair > 0:
                    gate = state if done else (k_first, v_first)
                    outgoing = lax.optimization_barrier((*outgoing, *gate))[:2]
                sent += outgoing
                k_parts[k_at ^ k_step] = exchange(outgoing[0], k_step)
                v_parts[v_at ^ v_step] = exchange(outgoing[1], v_step)
                done += 1
        k_parts.update({0: keys, steps[0]: k_first})
        v_parts.update({0: values, back[0]: v_first})
        if pair == 0:
            glob[0] = own
            for at in range(1, count):
                carrier = glob[at] if at in direct else v_parts[at] if at & steps[0] else k_parts[at]
                carrier = lax.optimization_barrier((carrier, *sent))[0]
                glob[at] = carrier if at in direct else carrier[tokens, :gpd].astype(jnp.int32)
            glob = jnp.concatenate([glob[at] + at * blocks for at in range(count)])
        else:
            window = lax.optimization_barrier((window, out))[0]
        state = call("early", pair, k_parts, v_parts, 3, window, row)
        spare = glob[gpd * last] - last * blocks
        out = call("late", pair, k_parts, v_parts, 1, halo, spare, state, out)
    return out


def solution(mesh):
    in_specs = (
        P(("batch", "seq"), "head"),
        P(("batch", "seq"), "head"),
        P(("batch", "seq"), "head"),
        P(("batch", "seq"), "head", None),
        P(("batch", "seq")),
    )
    out_specs = P(("batch", "seq"), "head")
    return jax.shard_map(shards, mesh=mesh, in_specs=in_specs, out_specs=out_specs, check_vma=False)
```

```python
import functools

import jax
import jax.numpy as jnp
from jax import lax
from jax.experimental import pallas as pl
from jax.experimental.pallas import tpu as pltpu
from jax.sharding import PartitionSpec as P

DH = 64
BLK = 64
RAND = 3
LANES = 2 * DH
ROWS = 16
TOGETHER = 8
ID_ROWS = 16
TOGETHER = 8
CHUNK = 2048
SUBS = 2
VMEM_BYTES = 16 * 1024 * 1024
EXP2_SCALE = 0.125 * 1.4426950408889634


def qk(q, k):
    return lax.dot_general(q, k, (((1,), (1,)), ((), ())), preferred_element_type=jnp.float32)


def part_kernel(
    pair, kind, wide, gpd, tokens, shared, lists_ref, flags_ref, glob_ref, own_ref, q_ref, *refs
):
    ranges = len(wide)
    blocks = tokens // BLK
    globs = gpd * ranges
    k_parts, v_parts, refs = refs[:ranges], refs[ranges : 2 * ranges], refs[2 * ranges :]
    if kind == "late":
        q_all, state_o_ref, state_l_ref = q_ref, *refs[:2]
        out_ref, k_glob, v_glob = refs[3:] if pair > 0 else refs[2:]
        k_all, v_all = k_parts[0], v_parts[0]
    else:
        out_ref, out_l_ref, q_all, k_glob, v_glob, k_all, v_all, sems = refs
        lanes = pl.ds(pair * LANES, LANES)
        copies = [pltpu.make_async_copy(q_ref.at[:, lanes], q_all, sems.at[2 * ranges])]
        for j in range(ranges):
            span = pl.ds(j * tokens, tokens)
            for side, (source, target) in enumerate(((k_parts[j], k_all), (v_parts[j], v_all))):
                source = source.at[:tokens, lanes] if wide[j][side] else source.at[:tokens]
                copies.append(pltpu.make_async_copy(source, target.at[span], sems.at[2 * j + side]))
        for copy in copies:
            copy.start()
        for copy in copies:
            copy.wait()

    first = lax.broadcasted_iota(jnp.int32, (BLK, LANES), 1) < DH
    first_few = lax.broadcasted_iota(jnp.int32, (16, LANES), 1) < DH
    block_ones = jnp.ones((BLK, LANES), jnp.bfloat16)

    def split_heads(q):
        zero = jnp.zeros_like(q)
        return [jnp.where(first, q, zero), jnp.where(first, zero, q)]

    def block(ref, position):
        return ref[pl.ds(pl.multiple_of(position * BLK, BLK), BLK), :]

    def listed(flag_a, flag_b):
        few = jnp.where(first_few, flag_a, flag_b).astype(jnp.bfloat16)
        return jnp.concatenate([few] * (BLK // 16), axis=0)

    def weighted(p, v, ones):
        return jnp.dot(
            p.astype(jnp.bfloat16), jnp.concatenate([v, ones], axis=1),
            preferred_element_type=jnp.float32,
        )

    def fold(rows):
        return jnp.where(first, rows[:BLK], rows[BLK:])

    def finish(b, target, peak, sums):
        o, total = fold(sums[:, :LANES]), fold(sums[:, LANES:])
        where = pl.ds(pl.multiple_of(target * BLK, BLK), BLK)
        top = fold(jnp.broadcast_to(peak, (2 * BLK, LANES))) * EXP2_SCALE
        if kind == "late":
            old_o, old_l = block(state_o_ref, b), block(state_l_ref, b)
            level = jnp.maximum(top, old_l)
            old_factor, factor = jnp.exp2(old_l - level), jnp.exp2(top - level)
            o = (old_o * old_factor + o * factor) / (old_factor + total * factor)
            out_ref[where, :] = o.astype(jnp.bfloat16)
        else:
            out_ref[where, :] = o / total
            out_l_ref[where, :] = top + jnp.log2(total)

    for g in range(globs):
        k_glob[g * BLK : (g + 1) * BLK, :] = block(k_all, glob_ref[g])
        v_glob[g * BLK : (g + 1) * BLK, :] = block(v_all, glob_ref[g])

    slots = shared + 2 * RAND

    glob_ones = jnp.ones((globs * BLK, LANES), jnp.bfloat16)

    def parts_of(row):
        at = row * slots
        q_bd = jnp.concatenate(split_heads(block(q_all, row)), axis=0)
        k_list, v_list, one_list = [], [], []
        for j in range(shared + RAND):
            a, b = (at + j, at + j) if j < shared else (at + j, at + RAND + j)
            k, v = block(k_all, lists_ref[a]), block(v_all, lists_ref[a])
            if j >= shared:
                k = jnp.where(first, k, block(k_all, lists_ref[b]))
                v = jnp.where(first, v, block(v_all, lists_ref[b]))
            if kind == "early" and j == 1:
                ones = block_ones
            else:
                ones = listed(flags_ref[a], flags_ref[b])
                v = v * ones
            k_list.append(k)
            v_list.append(v)
            one_list.append(ones)
        return q_bd, k_list, v_list, one_list

    def joined(arrays):
        return jnp.concatenate(arrays, axis=0)

    def scores(row):
        q_bd, k_list, v_list, one_list = parts_of(row)
        s = qk(q_bd, joined(k_list + [k_glob[...]]))
        return s, joined(v_list + [v_glob[...]]), joined(one_list + [glob_ones])

    def early_rows(step, carry):
        base = step * ROWS
        ahead = scores(base)
        for u in range(ROWS):
            (s, v, ones), ahead = ahead, scores(base + u + 1) if u + 1 < ROWS else None
            peak = jnp.max(s, axis=1, keepdims=True)
            w = jnp.exp2((s - peak) * EXP2_SCALE)
            finish(base + u, base + u, peak, weighted(w, v, ones))
        return carry

    def late_rows(base):
        rows = [parts_of(base + u) for u in range(TOGETHER)]
        s_own = [qk(q_bd, joined(k_list)) for q_bd, k_list, _, _ in rows]
        s_glob = qk(joined([q_bd for q_bd, _, _, _ in rows]), k_glob[...])
        sums, w_glob, peaks = [], [], []
        for u, (_, _, v_list, one_list) in enumerate(rows):
            s_here = s_glob[2 * BLK * u : 2 * BLK * (u + 1)]
            peak = jnp.maximum(
                jnp.max(s_own[u], axis=1, keepdims=True), jnp.max(s_here, axis=1, keepdims=True)
            )
            w = jnp.exp2((s_own[u] - peak) * EXP2_SCALE)
            sums.append(weighted(w, joined(v_list), joined(one_list)))
            w_glob.append(jnp.exp2((s_here - peak) * EXP2_SCALE).astype(jnp.bfloat16))
            peaks.append(peak)
        sums_glob = weighted(joined(w_glob), v_glob[...], glob_ones)
        for u in range(TOGETHER):
            here = sums_glob[2 * BLK * u : 2 * BLK * (u + 1)]
            finish(base + u, base + u, peaks[u], sums[u] + here)

    if kind == "late":
        for base in range(0, blocks, TOGETHER):
            late_rows(base)
    else:
        lax.fori_loop(0, blocks // ROWS, early_rows, 0)

    q_glob = []
    for g in range(gpd):
        q_glob += split_heads(block(q_all, own_ref[g]))
    q_glob = jnp.concatenate(q_glob, axis=0)
    chunk_ones = jnp.ones((CHUNK // SUBS, LANES), jnp.bfloat16)

    def chunk_step(c, carry):
        peak, sums = carry
        size = CHUNK // SUBS
        spans = [pl.ds(pl.multiple_of(c * CHUNK + i * size, size), size) for i in range(SUBS)]
        ahead = qk(q_glob, k_all[spans[0], :])
        for i in range(SUBS):
            s, ahead = ahead, qk(q_glob, k_all[spans[i + 1], :]) if i + 1 < SUBS else None
            top = jnp.maximum(peak, jnp.max(s, axis=1, keepdims=True))
            w = jnp.exp2((s - top) * EXP2_SCALE)
            factor = jnp.exp2((peak - top) * EXP2_SCALE)
            sums = sums * factor + weighted(w, v_all[spans[i], :], chunk_ones)
            peak = top
        return peak, sums

    height = 2 * gpd * BLK
    initial = (
        jnp.full((height, 1), -1e30, jnp.float32),
        jnp.zeros((height, 2 * LANES), jnp.float32),
    )
    peak, sums = lax.fori_loop(0, ranges * tokens // CHUNK, chunk_step, initial)
    for g in range(gpd):
        part = slice(2 * BLK * g, 2 * BLK * (g + 1))
        target = blocks + g if kind == "early" else own_ref[g]
        finish(blocks + g, target, peak[part], sums[part])


def part_call(
    pair, kind, shared, lists, flags, glob, own, queries, k_parts, v_parts, state=(), so_far=None
):
    tokens, columns = queries.shape
    if kind == "late":
        *state, queries = state
    ranges = len(k_parts)
    gpd = own.shape[0]
    smem = pl.BlockSpec(memory_space=pltpu.SMEM)
    hbm = pl.BlockSpec(memory_space=pltpu.HBM)
    half = pl.BlockSpec((tokens, LANES), lambda i: (0, pair))
    state_rows = tokens + gpd * BLK

    def full(rows):
        return pl.BlockSpec((rows, LANES), lambda i: (0, 0))

    operands = [lists, flags, glob, own, queries, *k_parts, *v_parts, *state]
    in_specs = [smem] * 4 + [full(tokens) if kind == "late" else hbm] * (1 + 2 * ranges)
    in_specs += [full(state_rows)] * len(state)
    aliases = {}
    if so_far is not None:
        aliases = {len(operands): 0}
        operands.append(so_far)
        in_specs.append(hbm)
    if kind == "early":
        out_specs = [full(state_rows)] * 2 + [full(tokens)]
        out_shape = [jax.ShapeDtypeStruct((state_rows, LANES), jnp.float32)] * 2
        out_shape.append(jax.ShapeDtypeStruct((tokens, LANES), queries.dtype))
    else:
        out_specs = half
        out_shape = jax.ShapeDtypeStruct((tokens, columns), jnp.bfloat16)
    keys_all = ranges * tokens
    globs = gpd * ranges * BLK
    pairs_done = 2 * tokens * ((shared + RAND) * BLK + globs) + 2 * gpd * BLK * keys_all
    wide = tuple((k.shape[1] > LANES, v.shape[1] > LANES) for k, v in zip(k_parts, v_parts))
    scratch = [pltpu.VMEM((globs, LANES), jnp.bfloat16)] * 2
    if kind != "late":
        scratch += [pltpu.VMEM((keys_all, LANES), jnp.bfloat16)] * 2
        scratch.append(pltpu.SemaphoreType.DMA((2 * ranges + 1,)))
    return pl.pallas_call(
        functools.partial(part_kernel, pair, kind, wide, gpd, tokens, shared),
        grid=(1,),
        in_specs=in_specs,
        out_specs=out_specs,
        out_shape=out_shape,
        input_output_aliases=aliases,
        scratch_shapes=scratch,
        compiler_params=pltpu.CompilerParams(vmem_limit_bytes=VMEM_BYTES + 8 * keys_all * LANES),
        cost_estimate=pl.CostEstimate(
            flops=16 * DH * pairs_done,
            bytes_accessed=4 * keys_all * LANES,
            transcendentals=pairs_done,
        ),
        name=kind,
    )(*operands)


def exchange(array, step):
    count = lax.axis_size("seq")
    return lax.ppermute(array, "seq", [(i, i ^ step) for i in range(count)])


def shards(queries, keys, values, rand_blocks, global_blocks):
    tokens, columns = queries.shape
    blocks = tokens // BLK
    gpd = global_blocks.shape[0]
    count = lax.axis_size("seq")
    rank = lax.axis_index("seq")
    pairs = columns // LANES
    steps = [1 << i for i in range(count.bit_length() - 1)]
    last = count - 1

    def place(ids):
        return ((ids // blocks) ^ rank) * blocks + ids % blocks

    row = jnp.arange(blocks)[:, None]
    window = place((rank * blocks + row + jnp.arange(-1, 2)) % (count * blocks))
    rand = place(rand_blocks)

    back = steps[::-1]
    k_first, v_first = exchange(keys, steps[0]), exchange(values, back[0])
    k_held, v_held, own, rand, window = lax.optimization_barrier(
        (keys, values, global_blocks - rank * blocks, rand, window)
    )
    id_rows = jnp.pad(own[None].astype(keys.dtype), ((0, ID_ROWS - 1), (0, LANES - gpd)))
    direct = [at for at in range(count) if at & steps[0] and at & back[0]]
    glob = {at: exchange(own, at) for at in direct}
    halo = jnp.where(row == 0, window[:, :1], window[:, 2:])

    def call(kind, pair, k_parts, v_parts, shared, listed, spare, state=(), so_far=None):
        start, stop = (last, count) if kind == "late" else (0, last)
        mine = rand[:, 2 * pair : 2 * pair + 2].reshape(blocks, 2 * RAND)
        lists = jnp.concatenate([listed, mine], axis=1)
        inside = (lists >= start * blocks) & (lists < stop * blocks)
        lists = jnp.where(inside, lists - start * blocks, spare)
        return part_call(
            pair, kind, shared, lists.reshape(-1), inside.astype(jnp.float32).reshape(-1),
            glob[gpd * start : gpd * stop] - start * blocks, own, queries,
            [k_parts[at] for at in range(start, stop)], [v_parts[at] for at in range(start, stop)],
            state, so_far,
        )

    out, state = None, None
    for pair in range(pairs):
        lanes = slice(pair * LANES, (pair + 1) * LANES)
        k_parts = {0: k_held[:, lanes], steps[0]: k_first[:, lanes]}
        v_parts = {0: v_held[:, lanes], back[0]: v_first[:, lanes]}
        if pair == 0:
            k_parts[0] = jnp.concatenate([k_parts[0], id_rows])
            v_parts[0] = jnp.concatenate([v_parts[0], id_rows])
        done, sent = 0, []
        for k_step, v_step in zip(steps[1:], back[1:]):
            for k_at, v_at in list(zip(k_parts, v_parts)):
                outgoing = (k_parts[k_at], v_parts[v_at])
                if pair > 0:
                    gate = state if done else (k_first, v_first)
                    outgoing = lax.optimization_barrier((*outgoing, *gate))[:2]
                sent += outgoing
                k_parts[k_at ^ k_step] = exchange(outgoing[0], k_step)
                v_parts[v_at ^ v_step] = exchange(outgoing[1], v_step)
                done += 1
        k_parts[steps[0]], v_parts[back[0]] = k_first, v_first
        if pair == 0:
            k_parts[0], v_parts[0] = keys, values
        if pair == 0:
            glob[0] = own
            for at in range(1, count):
                carrier = glob[at] if at in direct else v_parts[at] if at & steps[0] else k_parts[at]
                carrier = lax.optimization_barrier((carrier, *sent))[0]
                glob[at] = carrier if at in direct else carrier[tokens, :gpd].astype(jnp.int32)
            glob = jnp.concatenate([glob[at] + at * blocks for at in range(count)])
        else:
            window = lax.optimization_barrier((window, out))[0]
        state = call("early", pair, k_parts, v_parts, 3, window, row)
        spare = glob[gpd * last] - last * blocks
        out = call("late", pair, k_parts, v_parts, 1, halo, spare, state, out)
    return out


def solution(mesh):
    in_specs = (
        P(("batch", "seq"), "head"),
        P(("batch", "seq"), "head"),
        P(("batch", "seq"), "head"),
        P(("batch", "seq"), "head", None),
        P(("batch", "seq")),
    )
    out_specs = P(("batch", "seq"), "head")
    return jax.shard_map(shards, mesh=mesh, in_specs=in_specs, out_specs=out_specs, check_vma=False)
```

```python
import functools

import jax
import jax.numpy as jnp
from jax import lax
from jax.experimental import pallas as pl
from jax.experimental.pallas import tpu as pltpu
from jax.sharding import PartitionSpec as P

DH = 64
BLK = 64
RAND = 3
LANES = 2 * DH
ROWS = 16
TOGETHER = 8
ID_ROWS = 16
TOGETHER = 8
CHUNK = 2048
SUBS = 2
VMEM_BYTES = 16 * 1024 * 1024
EXP2_SCALE = 0.125 * 1.4426950408889634


def qk(q, k):
    return lax.dot_general(q, k, (((1,), (1,)), ((), ())), preferred_element_type=jnp.float32)


def part_kernel(
    pair, kind, wide, gpd, tokens, shared, lists_ref, flags_ref, glob_ref, own_ref, q_ref, *refs
):
    ranges = len(wide)
    blocks = tokens // BLK
    globs = gpd * ranges
    k_parts, v_parts, refs = refs[:ranges], refs[ranges : 2 * ranges], refs[2 * ranges :]
    if kind == "late":
        q_all, state_o_ref, state_l_ref = q_ref, *refs[:2]
        out_ref, k_glob, v_glob = refs[3:] if pair > 0 else refs[2:]
        k_all, v_all = k_parts[0], v_parts[0]
    else:
        out_ref, out_l_ref, q_all, *q_next, k_glob, v_glob, k_all, v_all, sems = refs
        lanes = pl.ds(pair * LANES, LANES)
        if pair == 0:
            q_halves = [q_ref.at[:, lanes], q_ref.at[:, pl.ds(LANES, LANES)]]
        else:
            q_halves = [q_ref]
        copies = [
            pltpu.make_async_copy(source, target, sems.at[2 * ranges + i])
            for i, (source, target) in enumerate(zip(q_halves, [q_all, *q_next]))
        ]
        for j in range(ranges):
            span = pl.ds(j * tokens, tokens)
            for side, (source, target) in enumerate(((k_parts[j], k_all), (v_parts[j], v_all))):
                source = source.at[:tokens, lanes] if wide[j][side] else source.at[:tokens]
                copies.append(pltpu.make_async_copy(source, target.at[span], sems.at[2 * j + side]))
        for copy in copies:
            copy.start()
        for copy in copies:
            copy.wait()

    first = lax.broadcasted_iota(jnp.int32, (BLK, LANES), 1) < DH
    first_few = lax.broadcasted_iota(jnp.int32, (16, LANES), 1) < DH
    block_ones = jnp.ones((BLK, LANES), jnp.bfloat16)

    def split_heads(q):
        zero = jnp.zeros_like(q)
        return [jnp.where(first, q, zero), jnp.where(first, zero, q)]

    def block(ref, position):
        return ref[pl.ds(pl.multiple_of(position * BLK, BLK), BLK), :]

    def listed(flag_a, flag_b):
        few = jnp.where(first_few, flag_a, flag_b).astype(jnp.bfloat16)
        return jnp.concatenate([few] * (BLK // 16), axis=0)

    def weighted(p, v, ones):
        return jnp.dot(
            p.astype(jnp.bfloat16), jnp.concatenate([v, ones], axis=1),
            preferred_element_type=jnp.float32,
        )

    def fold(rows):
        return jnp.where(first, rows[:BLK], rows[BLK:])

    def finish(b, target, peak, sums):
        o, total = fold(sums[:, :LANES]), fold(sums[:, LANES:])
        where = pl.ds(pl.multiple_of(target * BLK, BLK), BLK)
        top = fold(jnp.broadcast_to(peak, (2 * BLK, LANES))) * EXP2_SCALE
        if kind == "late":
            old_o, old_l = block(state_o_ref, b), block(state_l_ref, b)
            level = jnp.maximum(top, old_l)
            old_factor, factor = jnp.exp2(old_l - level), jnp.exp2(top - level)
            o = (old_o * old_factor + o * factor) / (old_factor + total * factor)
            out_ref[where, :] = o.astype(jnp.bfloat16)
        else:
            out_ref[where, :] = o / total
            out_l_ref[where, :] = top + jnp.log2(total)

    for g in range(globs):
        k_glob[g * BLK : (g + 1) * BLK, :] = block(k_all, glob_ref[g])
        v_glob[g * BLK : (g + 1) * BLK, :] = block(v_all, glob_ref[g])

    slots = shared + 2 * RAND

    glob_ones = jnp.ones((globs * BLK, LANES), jnp.bfloat16)

    def parts_of(row):
        at = row * slots
        q_bd = jnp.concatenate(split_heads(block(q_all, row)), axis=0)
        k_list, v_list, one_list = [], [], []
        for j in range(shared + RAND):
            a, b = (at + j, at + j) if j < shared else (at + j, at + RAND + j)
            k, v = block(k_all, lists_ref[a]), block(v_all, lists_ref[a])
            if j >= shared:
                k = jnp.where(first, k, block(k_all, lists_ref[b]))
                v = jnp.where(first, v, block(v_all, lists_ref[b]))
            if kind == "early" and j == 1:
                ones = block_ones
            else:
                ones = listed(flags_ref[a], flags_ref[b])
                v = v * ones
            k_list.append(k)
            v_list.append(v)
            one_list.append(ones)
        return q_bd, k_list, v_list, one_list

    def joined(arrays):
        return jnp.concatenate(arrays, axis=0)

    def scores(row):
        q_bd, k_list, v_list, one_list = parts_of(row)
        s = qk(q_bd, joined(k_list + [k_glob[...]]))
        return s, joined(v_list + [v_glob[...]]), joined(one_list + [glob_ones])

    def early_rows(step, carry):
        base = step * ROWS
        ahead = scores(base)
        for u in range(ROWS):
            (s, v, ones), ahead = ahead, scores(base + u + 1) if u + 1 < ROWS else None
            peak = jnp.max(s, axis=1, keepdims=True)
            w = jnp.exp2((s - peak) * EXP2_SCALE)
            finish(base + u, base + u, peak, weighted(w, v, ones))
        return carry

    def late_rows(base):
        rows = [parts_of(base + u) for u in range(TOGETHER)]
        s_own = [qk(q_bd, joined(k_list)) for q_bd, k_list, _, _ in rows]
        s_glob = qk(joined([q_bd for q_bd, _, _, _ in rows]), k_glob[...])
        sums, w_glob, peaks = [], [], []
        for u, (_, _, v_list, one_list) in enumerate(rows):
            s_here = s_glob[2 * BLK * u : 2 * BLK * (u + 1)]
            peak = jnp.maximum(
                jnp.max(s_own[u], axis=1, keepdims=True), jnp.max(s_here, axis=1, keepdims=True)
            )
            w = jnp.exp2((s_own[u] - peak) * EXP2_SCALE)
            sums.append(weighted(w, joined(v_list), joined(one_list)))
            w_glob.append(jnp.exp2((s_here - peak) * EXP2_SCALE).astype(jnp.bfloat16))
            peaks.append(peak)
        sums_glob = weighted(joined(w_glob), v_glob[...], glob_ones)
        for u in range(TOGETHER):
            here = sums_glob[2 * BLK * u : 2 * BLK * (u + 1)]
            finish(base + u, base + u, peaks[u], sums[u] + here)

    if kind == "late":
        for base in range(0, blocks, TOGETHER):
            late_rows(base)
    else:
        lax.fori_loop(0, blocks // ROWS, early_rows, 0)

    q_glob = []
    for g in range(gpd):
        q_glob += split_heads(block(q_all, own_ref[g]))
    q_glob = jnp.concatenate(q_glob, axis=0)
    chunk_ones = jnp.ones((CHUNK // SUBS, LANES), jnp.bfloat16)

    def chunk_step(c, carry):
        peak, sums = carry
        size = CHUNK // SUBS
        spans = [pl.ds(pl.multiple_of(c * CHUNK + i * size, size), size) for i in range(SUBS)]
        ahead = qk(q_glob, k_all[spans[0], :])
        for i in range(SUBS):
            s, ahead = ahead, qk(q_glob, k_all[spans[i + 1], :]) if i + 1 < SUBS else None
            top = jnp.maximum(peak, jnp.max(s, axis=1, keepdims=True))
            w = jnp.exp2((s - top) * EXP2_SCALE)
            factor = jnp.exp2((peak - top) * EXP2_SCALE)
            sums = sums * factor + weighted(w, v_all[spans[i], :], chunk_ones)
            peak = top
        return peak, sums

    height = 2 * gpd * BLK
    initial = (
        jnp.full((height, 1), -1e30, jnp.float32),
        jnp.zeros((height, 2 * LANES), jnp.float32),
    )
    peak, sums = lax.fori_loop(0, ranges * tokens // CHUNK, chunk_step, initial)
    for g in range(gpd):
        part = slice(2 * BLK * g, 2 * BLK * (g + 1))
        target = blocks + g if kind == "early" else own_ref[g]
        finish(blocks + g, target, peak[part], sums[part])


def part_call(
    pair, kind, shared, lists, flags, glob, own, queries, k_parts, v_parts, state=(), so_far=None
):
    tokens, columns = queries.shape
    if kind == "late":
        *state, queries = state
    ranges = len(k_parts)
    gpd = own.shape[0]
    smem = pl.BlockSpec(memory_space=pltpu.SMEM)
    hbm = pl.BlockSpec(memory_space=pltpu.HBM)
    half = pl.BlockSpec((tokens, LANES), lambda i: (0, pair))
    state_rows = tokens + gpd * BLK

    def full(rows):
        return pl.BlockSpec((rows, LANES), lambda i: (0, 0))

    operands = [lists, flags, glob, own, queries, *k_parts, *v_parts, *state]
    in_specs = [smem] * 4 + [full(tokens) if kind == "late" else hbm] * (1 + 2 * ranges)
    in_specs += [full(state_rows)] * len(state)
    aliases = {}
    if so_far is not None:
        aliases = {len(operands): 0}
        operands.append(so_far)
        in_specs.append(hbm)
    if kind == "early":
        handed = 2 if pair == 0 else 1
        out_specs = [full(state_rows)] * 2 + [full(tokens)] * handed
        out_shape = [jax.ShapeDtypeStruct((state_rows, LANES), jnp.float32)] * 2
        out_shape += [jax.ShapeDtypeStruct((tokens, LANES), queries.dtype)] * handed
    else:
        out_specs = half
        out_shape = jax.ShapeDtypeStruct((tokens, columns), jnp.bfloat16)
    keys_all = ranges * tokens
    globs = gpd * ranges * BLK
    pairs_done = 2 * tokens * ((shared + RAND) * BLK + globs) + 2 * gpd * BLK * keys_all
    wide = tuple((k.shape[1] > LANES, v.shape[1] > LANES) for k, v in zip(k_parts, v_parts))
    scratch = [pltpu.VMEM((globs, LANES), jnp.bfloat16)] * 2
    if kind != "late":
        scratch += [pltpu.VMEM((keys_all, LANES), jnp.bfloat16)] * 2
        scratch.append(pltpu.SemaphoreType.DMA((2 * ranges + 2,)))
    return pl.pallas_call(
        functools.partial(part_kernel, pair, kind, wide, gpd, tokens, shared),
        grid=(1,),
        in_specs=in_specs,
        out_specs=out_specs,
        out_shape=out_shape,
        input_output_aliases=aliases,
        scratch_shapes=scratch,
        compiler_params=pltpu.CompilerParams(vmem_limit_bytes=VMEM_BYTES + 8 * keys_all * LANES),
        cost_estimate=pl.CostEstimate(
            flops=16 * DH * pairs_done,
            bytes_accessed=4 * keys_all * LANES,
            transcendentals=pairs_done,
        ),
        name=kind,
    )(*operands)


def exchange(array, step):
    count = lax.axis_size("seq")
    return lax.ppermute(array, "seq", [(i, i ^ step) for i in range(count)])


def shards(queries, keys, values, rand_blocks, global_blocks):
    tokens, columns = queries.shape
    blocks = tokens // BLK
    gpd = global_blocks.shape[0]
    count = lax.axis_size("seq")
    rank = lax.axis_index("seq")
    pairs = columns // LANES
    steps = [1 << i for i in range(count.bit_length() - 1)]
    last = count - 1

    def place(ids):
        return ((ids // blocks) ^ rank) * blocks + ids % blocks

    row = jnp.arange(blocks)[:, None]
    window = place((rank * blocks + row + jnp.arange(-1, 2)) % (count * blocks))
    rand = place(rand_blocks)

    back = steps[::-1]
    k_first, v_first = exchange(keys, steps[0]), exchange(values, back[0])
    k_held, v_held, own, rand, window = lax.optimization_barrier(
        (keys, values, global_blocks - rank * blocks, rand, window)
    )
    id_rows = jnp.pad(own[None].astype(keys.dtype), ((0, ID_ROWS - 1), (0, LANES - gpd)))
    direct = [at for at in range(count) if at & steps[0] and at & back[0]]
    glob = {at: exchange(own, at) for at in direct}
    halo = jnp.where(row == 0, window[:, :1], window[:, 2:])

    def call(kind, pair, queries, k_parts, v_parts, shared, listed, spare, state=(), so_far=None):
        start, stop = (last, count) if kind == "late" else (0, last)
        mine = rand[:, 2 * pair : 2 * pair + 2].reshape(blocks, 2 * RAND)
        lists = jnp.concatenate([listed, mine], axis=1)
        inside = (lists >= start * blocks) & (lists < stop * blocks)
        lists = jnp.where(inside, lists - start * blocks, spare)
        return part_call(
            pair, kind, shared, lists.reshape(-1), inside.astype(jnp.float32).reshape(-1),
            glob[gpd * start : gpd * stop] - start * blocks, own, queries,
            [k_parts[at] for at in range(start, stop)], [v_parts[at] for at in range(start, stop)],
            state, so_far,
        )

    out, state, mine = None, None, queries
    for pair in range(pairs):
        lanes = slice(pair * LANES, (pair + 1) * LANES)
        k_parts = {0: k_held[:, lanes], steps[0]: k_first[:, lanes]}
        v_parts = {0: v_held[:, lanes], back[0]: v_first[:, lanes]}
        if pair == 0:
            k_parts[0] = jnp.concatenate([k_parts[0], id_rows])
            v_parts[0] = jnp.concatenate([v_parts[0], id_rows])
        done, sent = 0, []
        for k_step, v_step in zip(steps[1:], back[1:]):
            for k_at, v_at in list(zip(k_parts, v_parts)):
                outgoing = (k_parts[k_at], v_parts[v_at])
                if pair > 0:
                    gate = state if done else (k_first, v_first)
                    outgoing = lax.optimization_barrier((*outgoing, *gate))[:2]
                sent += outgoing
                k_parts[k_at ^ k_step] = exchange(outgoing[0], k_step)
                v_parts[v_at ^ v_step] = exchange(outgoing[1], v_step)
                done += 1
        k_parts[steps[0]], v_parts[back[0]] = k_first, v_first
        if pair == 0:
            k_parts[0], v_parts[0] = keys, values
        if pair == 0:
            glob[0] = own
            for at in range(1, count):
                carrier = glob[at] if at in direct else v_parts[at] if at & steps[0] else k_parts[at]
                carrier = lax.optimization_barrier((carrier, *sent))[0]
                glob[at] = carrier if at in direct else carrier[tokens, :gpd].astype(jnp.int32)
            glob = jnp.concatenate([glob[at] + at * blocks for at in range(count)])
        else:
            window = lax.optimization_barrier((window, out))[0]
        *state, mine = call("early", pair, mine, k_parts, v_parts, 3, window, row)
        if pair > 0:
            state.append(mine)
        spare = glob[gpd * last] - last * blocks
        out = call("late", pair, queries, k_parts, v_parts, 1, halo, spare, state, out)
    return out


def solution(mesh):
    in_specs = (
        P(("batch", "seq"), "head"),
        P(("batch", "seq"), "head"),
        P(("batch", "seq"), "head"),
        P(("batch", "seq"), "head", None),
        P(("batch", "seq")),
    )
    out_specs = P(("batch", "seq"), "head")
    return jax.shard_map(shards, mesh=mesh, in_specs=in_specs, out_specs=out_specs, check_vma=False)
```

```python
import functools

import jax
import jax.numpy as jnp
from jax import lax
from jax.experimental import pallas as pl
from jax.experimental.pallas import tpu as pltpu
from jax.sharding import PartitionSpec as P

DH = 64
BLK = 64
RAND = 3
LANES = 2 * DH
ROWS = 16
TOGETHER = 8
ID_ROWS = 16
TOGETHER = 8
CHUNK = 2048
SUBS = 2
VMEM_BYTES = 8 * 1024 * 1024
EXP2_SCALE = 0.125 * 1.4426950408889634


def qk(q, k):
    return lax.dot_general(q, k, (((1,), (1,)), ((), ())), preferred_element_type=jnp.float32)


def part_kernel(
    pair, kind, wide, gpd, tokens, shared, lists_ref, flags_ref, glob_ref, own_ref, q_ref, *refs
):
    ranges = len(wide)
    blocks = tokens // BLK
    globs = gpd * ranges
    k_parts, v_parts, refs = refs[:ranges], refs[ranges : 2 * ranges], refs[2 * ranges :]
    if kind == "late":
        q_all, state_o_ref, state_l_ref = q_ref, *refs[:2]
        out_ref, k_glob, v_glob = refs[3:] if pair > 0 else refs[2:]
        k_all, v_all = k_parts[0], v_parts[0]
    else:
        out_ref, out_l_ref, q_all, *q_next, k_glob, v_glob, k_all, v_all, sems = refs
        lanes = pl.ds(pair * LANES, LANES)
        if pair == 0:
            q_halves = [q_ref.at[:, lanes], q_ref.at[:, pl.ds(LANES, LANES)]]
        else:
            q_halves = [q_ref]
        copies = [
            pltpu.make_async_copy(source, target, sems.at[2 * ranges + i])
            for i, (source, target) in enumerate(zip(q_halves, [q_all, *q_next]))
        ]
        for j in range(ranges):
            span = pl.ds(j * tokens, tokens)
            for side, (source, target) in enumerate(((k_parts[j], k_all), (v_parts[j], v_all))):
                source = source.at[:tokens, lanes] if wide[j][side] else source.at[:tokens]
                copies.append(pltpu.make_async_copy(source, target.at[span], sems.at[2 * j + side]))
        for copy in copies:
            copy.start()
        for copy in copies:
            copy.wait()

    first = lax.broadcasted_iota(jnp.int32, (BLK, LANES), 1) < DH
    first_few = lax.broadcasted_iota(jnp.int32, (16, LANES), 1) < DH
    block_ones = jnp.ones((BLK, LANES), jnp.bfloat16)

    def split_heads(q):
        zero = jnp.zeros_like(q)
        return [jnp.where(first, q, zero), jnp.where(first, zero, q)]

    def block(ref, position):
        return ref[pl.ds(pl.multiple_of(position * BLK, BLK), BLK), :]

    def listed(flag_a, flag_b):
        few = jnp.where(first_few, flag_a, flag_b).astype(jnp.bfloat16)
        return jnp.concatenate([few] * (BLK // 16), axis=0)

    def weighted(p, v, ones):
        return jnp.dot(
            p.astype(jnp.bfloat16), jnp.concatenate([v, ones], axis=1),
            preferred_element_type=jnp.float32,
        )

    def fold(rows):
        return jnp.where(first, rows[:BLK], rows[BLK:])

    def finish(b, target, peak, sums):
        o, total = fold(sums[:, :LANES]), fold(sums[:, LANES:])
        where = pl.ds(pl.multiple_of(target * BLK, BLK), BLK)
        top = fold(jnp.broadcast_to(peak, (2 * BLK, LANES))) * EXP2_SCALE
        if kind == "late":
            old_o, old_l = block(state_o_ref, b), block(state_l_ref, b)
            level = jnp.maximum(top, old_l)
            old_factor, factor = jnp.exp2(old_l - level), jnp.exp2(top - level)
            o = (old_o * old_factor + o * factor) / (old_factor + total * factor)
            out_ref[where, :] = o.astype(jnp.bfloat16)
        else:
            out_ref[where, :] = o / total
            out_l_ref[where, :] = top + jnp.log2(total)

    for g in range(globs):
        k_glob[g * BLK : (g + 1) * BLK, :] = block(k_all, glob_ref[g])
        v_glob[g * BLK : (g + 1) * BLK, :] = block(v_all, glob_ref[g])

    slots = shared + 2 * RAND

    glob_ones = jnp.ones((globs * BLK, LANES), jnp.bfloat16)

    def parts_of(row):
        at = row * slots
        q_bd = jnp.concatenate(split_heads(block(q_all, row)), axis=0)
        k_list, v_list, one_list = [], [], []
        for j in range(shared + RAND):
            a, b = (at + j, at + j) if j < shared else (at + j, at + RAND + j)
            k, v = block(k_all, lists_ref[a]), block(v_all, lists_ref[a])
            if j >= shared:
                k = jnp.where(first, k, block(k_all, lists_ref[b]))
                v = jnp.where(first, v, block(v_all, lists_ref[b]))
            if kind == "early" and j == 1:
                ones = block_ones
            else:
                ones = listed(flags_ref[a], flags_ref[b])
                v = v * ones
            k_list.append(k)
            v_list.append(v)
            one_list.append(ones)
        return q_bd, k_list, v_list, one_list

    def joined(arrays):
        return jnp.concatenate(arrays, axis=0)

    def scores(row):
        q_bd, k_list, v_list, one_list = parts_of(row)
        s = qk(q_bd, joined(k_list + [k_glob[...]]))
        return s, joined(v_list + [v_glob[...]]), joined(one_list + [glob_ones])

    def early_rows(step, carry):
        base = step * ROWS
        ahead = scores(base)
        for u in range(ROWS):
            (s, v, ones), ahead = ahead, scores(base + u + 1) if u + 1 < ROWS else None
            peak = jnp.max(s, axis=1, keepdims=True)
            w = jnp.exp2((s - peak) * EXP2_SCALE)
            finish(base + u, base + u, peak, weighted(w, v, ones))
        return carry

    def late_rows(base):
        rows = [parts_of(base + u) for u in range(TOGETHER)]
        s_own = [qk(q_bd, joined(k_list)) for q_bd, k_list, _, _ in rows]
        s_glob = qk(joined([q_bd for q_bd, _, _, _ in rows]), k_glob[...])
        sums, w_glob, peaks = [], [], []
        for u, (_, _, v_list, one_list) in enumerate(rows):
            s_here = s_glob[2 * BLK * u : 2 * BLK * (u + 1)]
            peak = jnp.maximum(
                jnp.max(s_own[u], axis=1, keepdims=True), jnp.max(s_here, axis=1, keepdims=True)
            )
            w = jnp.exp2((s_own[u] - peak) * EXP2_SCALE)
            sums.append(weighted(w, joined(v_list), joined(one_list)))
            w_glob.append(jnp.exp2((s_here - peak) * EXP2_SCALE).astype(jnp.bfloat16))
            peaks.append(peak)
        sums_glob = weighted(joined(w_glob), v_glob[...], glob_ones)
        for u in range(TOGETHER):
            here = sums_glob[2 * BLK * u : 2 * BLK * (u + 1)]
            finish(base + u, base + u, peaks[u], sums[u] + here)

    if kind == "late":
        for base in range(0, blocks, TOGETHER):
            late_rows(base)
    else:
        lax.fori_loop(0, blocks // ROWS, early_rows, 0)

    q_glob = []
    for g in range(gpd):
        q_glob += split_heads(block(q_all, own_ref[g]))
    q_glob = jnp.concatenate(q_glob, axis=0)
    chunk_ones = jnp.ones((CHUNK // SUBS, LANES), jnp.bfloat16)

    def chunk_step(c, carry):
        peak, sums = carry
        size = CHUNK // SUBS
        spans = [pl.ds(pl.multiple_of(c * CHUNK + i * size, size), size) for i in range(SUBS)]
        ahead = qk(q_glob, k_all[spans[0], :])
        for i in range(SUBS):
            s, ahead = ahead, qk(q_glob, k_all[spans[i + 1], :]) if i + 1 < SUBS else None
            top = jnp.maximum(peak, jnp.max(s, axis=1, keepdims=True))
            w = jnp.exp2((s - top) * EXP2_SCALE)
            factor = jnp.exp2((peak - top) * EXP2_SCALE)
            sums = sums * factor + weighted(w, v_all[spans[i], :], chunk_ones)
            peak = top
        return peak, sums

    height = 2 * gpd * BLK
    initial = (
        jnp.full((height, 1), -1e30, jnp.float32),
        jnp.zeros((height, 2 * LANES), jnp.float32),
    )
    peak, sums = lax.fori_loop(0, ranges * tokens // CHUNK, chunk_step, initial)
    for g in range(gpd):
        part = slice(2 * BLK * g, 2 * BLK * (g + 1))
        target = blocks + g if kind == "early" else own_ref[g]
        finish(blocks + g, target, peak[part], sums[part])


def part_call(
    pair, kind, shared, lists, flags, glob, own, queries, k_parts, v_parts, state=(), so_far=None
):
    tokens, columns = queries.shape
    if kind == "late":
        *state, queries = state
    ranges = len(k_parts)
    gpd = own.shape[0]
    smem = pl.BlockSpec(memory_space=pltpu.SMEM)
    hbm = pl.BlockSpec(memory_space=pltpu.HBM)
    half = pl.BlockSpec((tokens, LANES), lambda i: (0, pair))
    state_rows = tokens + gpd * BLK

    def full(rows):
        return pl.BlockSpec((rows, LANES), lambda i: (0, 0))

    operands = [lists, flags, glob, own, queries, *k_parts, *v_parts, *state]
    in_specs = [smem] * 4 + [full(tokens) if kind == "late" else hbm] * (1 + 2 * ranges)
    in_specs += [full(state_rows)] * len(state)
    aliases = {}
    if so_far is not None:
        aliases = {len(operands): 0}
        operands.append(so_far)
        in_specs.append(hbm)
    if kind == "early":
        handed = 2 if pair == 0 else 1
        out_specs = [full(state_rows)] * 2 + [full(tokens)] * handed
        out_shape = [jax.ShapeDtypeStruct((state_rows, LANES), jnp.float32)] * 2
        out_shape += [jax.ShapeDtypeStruct((tokens, LANES), queries.dtype)] * handed
    else:
        out_specs = half
        out_shape = jax.ShapeDtypeStruct((tokens, columns), jnp.bfloat16)
    keys_all = ranges * tokens
    globs = gpd * ranges * BLK
    pairs_done = 2 * tokens * ((shared + RAND) * BLK + globs) + 2 * gpd * BLK * keys_all
    wide = tuple((k.shape[1] > LANES, v.shape[1] > LANES) for k, v in zip(k_parts, v_parts))
    scratch = [pltpu.VMEM((globs, LANES), jnp.bfloat16)] * 2
    if kind != "late":
        scratch += [pltpu.VMEM((keys_all, LANES), jnp.bfloat16)] * 2
        scratch.append(pltpu.SemaphoreType.DMA((2 * ranges + 2,)))
    return pl.pallas_call(
        functools.partial(part_kernel, pair, kind, wide, gpd, tokens, shared),
        grid=(1,),
        in_specs=in_specs,
        out_specs=out_specs,
        out_shape=out_shape,
        input_output_aliases=aliases,
        scratch_shapes=scratch,
        compiler_params=pltpu.CompilerParams(vmem_limit_bytes=VMEM_BYTES + 8 * keys_all * LANES),
        cost_estimate=pl.CostEstimate(
            flops=16 * DH * pairs_done,
            bytes_accessed=4 * keys_all * LANES,
            transcendentals=pairs_done,
        ),
        name=kind,
    )(*operands)


def exchange(array, step):
    count = lax.axis_size("seq")
    return lax.ppermute(array, "seq", [(i, i ^ step) for i in range(count)])


def shards(queries, keys, values, rand_blocks, global_blocks):
    tokens, columns = queries.shape
    blocks = tokens // BLK
    gpd = global_blocks.shape[0]
    count = lax.axis_size("seq")
    rank = lax.axis_index("seq")
    pairs = columns // LANES
    steps = [1 << i for i in range(count.bit_length() - 1)]
    last = count - 1

    def place(ids):
        return ((ids // blocks) ^ rank) * blocks + ids % blocks

    row = jnp.arange(blocks)[:, None]
    window = place((rank * blocks + row + jnp.arange(-1, 2)) % (count * blocks))
    rand = place(rand_blocks)

    back = steps[::-1]
    k_first, v_first = exchange(keys, steps[0]), exchange(values, back[0])
    k_held, v_held, own, rand, window = lax.optimization_barrier(
        (keys, values, global_blocks - rank * blocks, rand, window)
    )
    id_rows = jnp.pad(own[None].astype(keys.dtype), ((0, ID_ROWS - 1), (0, LANES - gpd)))
    direct = [at for at in range(count) if at & steps[0] and at & back[0]]
    glob = {at: exchange(own, at) for at in direct}
    halo = jnp.where(row == 0, window[:, :1], window[:, 2:])

    def call(kind, pair, queries, k_parts, v_parts, shared, listed, spare, state=(), so_far=None):
        start, stop = (last, count) if kind == "late" else (0, last)
        mine = rand[:, 2 * pair : 2 * pair + 2].reshape(blocks, 2 * RAND)
        lists = jnp.concatenate([listed, mine], axis=1)
        inside = (lists >= start * blocks) & (lists < stop * blocks)
        lists = jnp.where(inside, lists - start * blocks, spare)
        return part_call(
            pair, kind, shared, lists.reshape(-1), inside.astype(jnp.float32).reshape(-1),
            glob[gpd * start : gpd * stop] - start * blocks, own, queries,
            [k_parts[at] for at in range(start, stop)], [v_parts[at] for at in range(start, stop)],
            state, so_far,
        )

    out, state, mine = None, None, queries
    for pair in range(pairs):
        lanes = slice(pair * LANES, (pair + 1) * LANES)
        k_parts = {0: k_held[:, lanes], steps[0]: k_first[:, lanes]}
        v_parts = {0: v_held[:, lanes], back[0]: v_first[:, lanes]}
        if pair == 0:
            k_parts[0] = jnp.concatenate([k_parts[0], id_rows])
            v_parts[0] = jnp.concatenate([v_parts[0], id_rows])
        done, sent = 0, []
        for k_step, v_step in zip(steps[1:], back[1:]):
            for k_at, v_at in list(zip(k_parts, v_parts)):
                outgoing = (k_parts[k_at], v_parts[v_at])
                if pair > 0:
                    gate = state if done else (k_first, v_first)
                    outgoing = lax.optimization_barrier((*outgoing, *gate))[:2]
                sent += outgoing
                k_parts[k_at ^ k_step] = exchange(outgoing[0], k_step)
                v_parts[v_at ^ v_step] = exchange(outgoing[1], v_step)
                done += 1
        k_parts[steps[0]], v_parts[back[0]] = k_first, v_first
        if pair == 0:
            k_parts[0], v_parts[0] = keys, values
        if pair == 0:
            glob[0] = own
            for at in range(1, count):
                carrier = glob[at] if at in direct else v_parts[at] if at & steps[0] else k_parts[at]
                carrier = lax.optimization_barrier((carrier, *sent))[0]
                glob[at] = carrier if at in direct else carrier[tokens, :gpd].astype(jnp.int32)
            glob = jnp.concatenate([glob[at] + at * blocks for at in range(count)])
        else:
            window = lax.optimization_barrier((window, out))[0]
        *state, mine = call("early", pair, mine, k_parts, v_parts, 3, window, row)
        if pair > 0:
            state.append(mine)
        spare = glob[gpd * last] - last * blocks
        out = call("late", pair, queries, k_parts, v_parts, 1, halo, spare, state, out)
    return out


def solution(mesh):
    in_specs = (
        P(("batch", "seq"), "head"),
        P(("batch", "seq"), "head"),
        P(("batch", "seq"), "head"),
        P(("batch", "seq"), "head", None),
        P(("batch", "seq")),
    )
    out_specs = P(("batch", "seq"), "head")
    return jax.shard_map(shards, mesh=mesh, in_specs=in_specs, out_specs=out_specs, check_vma=False)
```
